512 devices in a mesh: dp: 8 (over z_hi, core), ctx: 64 (over x, y, z_lo).
Axes of the slice: x: 4, y: 8, z: 8 (z_hi: 4, z_lo: 2; z = z_hi * 2 + z_lo), core: 2. Of those that a mesh axis runs over, the one named last changes fastest.
Arguments:
- query_proj: bfloat16 [8, 8192, 2560], P('dp', 'ctx'), may hold values from -12 to 12
- key_proj: bfloat16 [8, 8192, 2560], P('dp', 'ctx'), may hold values from -12 to 12
- value_proj: bfloat16 [8, 8192, 2560], P('dp', 'ctx'), may hold values from -6 to 6
- out_grad: bfloat16 [8, 8192, 2560], P('dp', 'ctx'), may hold values from -20 to 20
- out_gain: float32 [2560], replicated, may hold values from 0.1 to 1.9
Outputs:
- grad_query: bfloat16 [8, 8192, 2560], P('dp', 'ctx')
- grad_key: bfloat16 [8, 8192, 2560], P('dp', 'ctx')
- grad_value: bfloat16 [8, 8192, 2560], P('dp', 'ctx')
- grad_gain: float32 [2560], replicated
The draws below stay inside these ranges and needn't reach their ends.
All inputs are finite; a program needn't handle non-finite values.
Results may differ from the reference program's by a relative error of at most 0.0058.
Values may be sent and summed in bfloat16 or wider, within the bound.
A program may use at most 64 MiB of HBM per device.

```python
import math
import jax
import jax.numpy as jnp
from jax import lax

HEADS = 20
HEAD_DIM = 128
BLOCK = 128
HD = 2560
TRAJ = 8
LENGTH = 8192


def draw_query_proj(key, part):
    key = jax.random.fold_in(key, 1)
    result = jnp.clip(jax.random.normal(key, (TRAJ, LENGTH, HD), jnp.float32), -4.0, 4.0)
    return result.astype(jnp.bfloat16)


def draw_key_proj(key, part):
    key = jax.random.fold_in(key, 2)
    result = jnp.clip(jax.random.normal(key, (TRAJ, LENGTH, HD), jnp.float32), -4.0, 4.0)
    return result.astype(jnp.bfloat16)


def draw_out_grad(key, part):
    key = jax.random.fold_in(key, 3)
    noise = jnp.clip(jax.random.normal(key, (TRAJ, LENGTH, HD), jnp.float32), -4.0, 4.0)
    position = jnp.arange(LENGTH).astype(jnp.float32)
    fraction = position / (LENGTH - 1)
    result = noise * (1.0 + 2.0 * fraction)[None, :, None]
    return result.astype(jnp.bfloat16)


def level_of(key, dims, split, smallest, top_value):
    gain, own = 1.0, jax.random.fold_in(key, 6)
    for dim, shards_of in split:
        steps = jnp.exp(jax.random.uniform(jax.random.fold_in(own, dim), (shards_of,), jnp.float32, smallest / len(split), top_value / len(split)))
        gain = gain * jnp.repeat(steps, dims[dim] // shards_of).reshape([-1 if axis == dim else 1 for axis in range(len(dims))])
    return gain


def normal_values(key, shape, width, limit, split=(), held_as=jnp.bfloat16):
    values = width * jax.random.normal(key, shape, jnp.float32)
    if split:
        values = values * level_of(key, shape, split, -0.22, 0.18)
    return jnp.clip(values, -limit, limit).astype(held_as)


def setup_inputs(seed: int = 0) -> dict:
    seeds = jax.random.split(jax.random.key(seed), 6)
    return {
        "query_proj": draw_query_proj(jax.random.fold_in(seeds[5], 71), 0),
        "key_proj": draw_key_proj(jax.random.fold_in(seeds[5], 71), 0),
        "value_proj": normal_values(seeds[2], (TRAJ, LENGTH, HD), 1.0, 6.0, ((0, 8), (1, 64))),
        "out_grad": draw_out_grad(jax.random.fold_in(seeds[5], 71), 0),
        "out_gain": jnp.clip(1.0 + 0.18 * jax.random.normal(seeds[4], (HD,), jnp.float32), 0.1, 1.9),
    }


def attend_one(query_proj, key_proj, value_proj, out_grad, out_gain):
    blocks = LENGTH // BLOCK
    score_scale = 1.0 / math.sqrt(HEAD_DIM)
    query_rows = query_proj.astype(jnp.float32).reshape(blocks, BLOCK, HEADS, HEAD_DIM)
    key_rows = key_proj.astype(jnp.float32).reshape(blocks, BLOCK, HEADS, HEAD_DIM)
    value_rows = value_proj.astype(jnp.float32).reshape(blocks, BLOCK, HEADS, HEAD_DIM)
    panel_key = key_rows[:, BLOCK - 1]
    panel_value = value_rows[:, BLOCK - 1]
    inner_ids = jnp.arange(BLOCK)
    local_keep = inner_ids[:, None] >= inner_ids[None, :]
    block_ids = jnp.arange(blocks)
    far_keep = block_ids[None, :] < block_ids[:, None]
    local_scores = jnp.einsum('bqhd,bkhd->bhqk', query_rows, key_rows) * score_scale
    far_scores = jnp.einsum('bqhd,shd->bhqs', query_rows, panel_key) * score_scale
    local_scores = jnp.where(local_keep[None, None], local_scores, -jnp.inf)
    far_scores = jnp.where(far_keep[:, None, None, :], far_scores, -jnp.inf)
    row_top = jnp.maximum(lax.optimization_barrier(jnp.max(local_scores, axis=-1, keepdims=True)), lax.optimization_barrier(jnp.max(far_scores, axis=-1, keepdims=True)))
    local_exp = jnp.exp(local_scores - row_top)
    far_exp = jnp.exp(far_scores - row_top)
    row_total = lax.optimization_barrier(jnp.sum(local_exp, axis=-1, keepdims=True)) + lax.optimization_barrier(jnp.sum(far_exp, axis=-1, keepdims=True))
    local_prob = local_exp / row_total
    far_prob = far_exp / row_total
    local_half = local_prob.astype(jnp.bfloat16).astype(jnp.float32)
    far_half = far_prob.astype(jnp.bfloat16).astype(jnp.float32)
    attended = jnp.einsum('bhqk,bkhd->bqhd', local_half, value_rows) + jnp.einsum('bhqs,shd->bqhd', far_half, panel_value)
    grad_rows = out_grad.astype(jnp.float32).reshape(blocks, BLOCK, HEADS, HEAD_DIM)
    gain_rows = out_gain.reshape(HEADS, HEAD_DIM)
    grad_attn = (grad_rows * gain_rows).astype(jnp.bfloat16).astype(jnp.float32)
    gain_part = lax.optimization_barrier(jnp.sum(grad_rows * attended, axis=(0, 1))).reshape(HD)
    local_dprob = jnp.einsum('bqhd,bkhd->bhqk', grad_attn, value_rows)
    far_dprob = jnp.einsum('bqhd,shd->bhqs', grad_attn, panel_value)
    row_dot = lax.optimization_barrier(jnp.sum(local_prob * local_dprob, axis=-1, keepdims=True)) + lax.optimization_barrier(jnp.sum(far_prob * far_dprob, axis=-1, keepdims=True))
    local_dscore = (local_prob * (local_dprob - row_dot)).astype(jnp.bfloat16).astype(jnp.float32)
    far_dscore = (far_prob * (far_dprob - row_dot)).astype(jnp.bfloat16).astype(jnp.float32)
    grad_query = (jnp.einsum('bhqk,bkhd->bqhd', local_dscore, key_rows) + jnp.einsum('bhqs,shd->bqhd', far_dscore, panel_key)) * score_scale
    local_gkey = jnp.einsum('bhqk,bqhd->bkhd', local_dscore, query_rows) * score_scale
    local_gvalue = jnp.einsum('bhqk,bqhd->bkhd', local_half, grad_attn)
    far_gkey = jnp.einsum('bhqs,bqhd->shd', far_dscore, query_rows) * score_scale
    far_gvalue = jnp.einsum('bhqs,bqhd->shd', far_half, grad_attn)
    grad_key = local_gkey.at[:, BLOCK - 1].add(far_gkey)
    grad_value = local_gvalue.at[:, BLOCK - 1].add(far_gvalue)
    return (grad_query.reshape(LENGTH, HD).astype(jnp.bfloat16), grad_key.reshape(LENGTH, HD).astype(jnp.bfloat16), grad_value.reshape(LENGTH, HD).astype(jnp.bfloat16), gain_part)

def reference(query_proj, key_proj, value_proj, out_grad, out_gain):

    def one_trajectory(members):
        return attend_one(members[0], members[1], members[2], members[3], out_gain)
    grad_query, grad_key, grad_value, gain_parts = lax.map(one_trajectory, (query_proj, key_proj, value_proj, out_grad))
    grad_gain = lax.optimization_barrier(jnp.sum(gain_parts, axis=0)) / TRAJ
    return (grad_query, grad_key, grad_value, grad_gain)
```

```python
import functools
import math

import jax
import jax.numpy as jnp
from jax import lax
from jax.experimental import pallas as pl
from jax.experimental.pallas import tpu as pltpu
from jax.sharding import PartitionSpec as P

DIM = 128
BLOCK = 128
NX, NY, NZ = 4, 8, 2
GROUPS = 2
MESH = pl.DeviceIdType.MESH
F32 = jnp.float32
BF16 = jnp.bfloat16


def dot(a, b, dims):
    return lax.dot_general(a, b, (dims, ((), ())), preferred_element_type=F32)


def kernel(
    heads, ndp,
    q_hbm, k_hbm, v_hbm, g_hbm, gain_ref,
    gq_hbm, gk_hbm, gv_hbm, gg_ref,
    qv, kc, vc, gv, gqo, gko, gvo, lastk, lastv, st, dpt,
    tails, send, rbuf, acc, pairs, asend, arecv, gpart, gb1, gb2, gb3,
    insem, outsem, a_s, a_r, b_s, b_r, c_s, c_r, d_s, d_r, g_s, g_r,
):
    features = heads * DIM
    plane = NY * NZ
    blocks = NX * plane
    scale = 1.0 / math.sqrt(DIM)
    escale = scale * math.log2(math.e)
    dp = lax.axis_index("dp")
    me = lax.axis_index("ctx")
    ip = lax.rem(me, plane)
    ix = lax.div(me, plane)
    iy = lax.div(ip, NZ)
    iz = lax.rem(ip, NZ)
    row0 = pl.multiple_of(BLOCK + ix * plane, plane)

    def ctx_of(x, y, z):
        return x * plane + y * NZ + z

    first = BLOCK - 16
    loads = []
    for n, (src, dst) in enumerate(((k_hbm, kc), (v_hbm, vc))):
        cp = pltpu.make_async_copy(src.at[pl.ds(first, 16)], dst.at[pl.ds(first, 16)], insem.at[n])
        cp.start()
        loads.append(cp)
    for n, (src, dst) in enumerate(((k_hbm, kc), (v_hbm, vc))):
        cp = pltpu.make_async_copy(src.at[pl.ds(0, first)], dst.at[pl.ds(0, first)], insem.at[2 + n])
        cp.start()
        loads.append(cp)
    for n, (src, dst) in enumerate(((q_hbm, qv), (g_hbm, gv))):
        cp = pltpu.make_async_copy(src, dst, insem.at[4 + n])
        cp.start()
        loads.append(cp)

    kc[BLOCK:] = jnp.zeros((blocks, features), BF16)
    vc[BLOCK:] = jnp.zeros((blocks, features), BF16)

    barrier = pltpu.get_barrier_semaphore()
    count = 0

    def greet(device):
        pl.semaphore_signal(barrier, inc=1, device_id=device, device_id_type=MESH)

    for j in range(1, plane):
        greet({"ctx": ix * plane + lax.rem(ip + j, plane)})
        count += 1
    for j in range(1, NX):
        for dz in range(NZ):
            greet({"ctx": ctx_of(lax.rem(ix + j, NX), iy, lax.rem(iz + dz, NZ))})
            count += 1
    for j in range(1, ndp):
        greet({"dp": lax.rem(dp + j, ndp)})
        count += 1

    loads[0].wait()
    loads[1].wait()
    ktail = kc[pl.ds(first, 16)].astype(F32)[15:16]
    vtail = vc[pl.ds(first, 16)].astype(F32)[15:16]
    tails[ip] = jnp.concatenate([ktail, vtail], axis=0).astype(BF16)

    pl.semaphore_wait(barrier, count)

    def a_copy(j):
        p = lax.rem(ip + j, plane)
        return pltpu.make_async_remote_copy(
            src_ref=tails.at[ip], dst_ref=tails.at[ip], send_sem=a_s.at[j], recv_sem=a_r.at[ip],
            device_id={"ctx": ix * plane + p}, device_id_type=MESH)

    def a_wait(j):
        p = lax.rem(ip + j, plane)
        pltpu.make_async_remote_copy(
            src_ref=tails.at[p], dst_ref=tails.at[p], send_sem=a_s.at[j], recv_sem=a_r.at[p],
            device_id={"ctx": ix * plane + p}, device_id_type=MESH).wait_recv()

    for j in range(1, plane):
        a_copy(j).start()

    for n in range(2, 6):
        loads[n].wait()

    key_id = lax.broadcasted_iota(jnp.int32, (BLOCK, BLOCK), 0)
    query_id = lax.broadcasted_iota(jnp.int32, (BLOCK, BLOCK), 1)
    far_id = lax.broadcasted_iota(jnp.int32, (blocks, BLOCK), 0)
    neg = -jnp.inf

    def cols(h, base=0):
        return pl.ds(pl.multiple_of(h * DIM + base, DIM), DIM)

    def local_part(h, _):
        c = cols(h)
        g = gv[:, c]
        ga = (g.astype(F32) * gain_ref[:, c]).astype(BF16)
        s = dot(kc[pl.ds(0, BLOCK), c], qv[:, c], ((1,), (1,)))
        st[h] = jnp.where(key_id <= query_id, s, neg)
        dpt[h] = dot(vc[pl.ds(0, BLOCK), c], ga, ((1,), (1,)))
        return 0

    half = heads // 2
    lax.fori_loop(0, half, local_part, 0)

    for j in range(1, plane):
        a_wait(j)
    for i in range(plane):
        pairs[pl.ds(2 * i, 2)] = tails[i].astype(F32)
    to_id = lax.broadcasted_iota(jnp.int32, (2 * plane, 2 * plane), 0)
    from_id = lax.broadcasted_iota(jnp.int32, (2 * plane, 2 * plane), 1)
    apart = jnp.where(from_id == 2 * lax.rem(to_id, plane) + lax.div(to_id, plane), 1.0, 0.0).astype(BF16)
    sorted_rows = dot(apart, pairs[...].astype(BF16), ((1,), (0,)))
    kc[pl.ds(row0, plane)] = sorted_rows[:plane].astype(BF16)
    vc[pl.ds(row0, plane)] = sorted_rows[plane:].astype(BF16)

    def b_copy(d, n, start):
        buf = (kc, vc)[n]
        row = start
        return pltpu.make_async_remote_copy(
            src_ref=buf.at[pl.ds(row, plane)], dst_ref=buf.at[pl.ds(row, plane)],
            send_sem=b_s.at[d, n], recv_sem=b_r.at[d, n],
            device_id={"ctx": lax.rem(ix + d, NX) * plane + ip}, device_id_type=MESH)

    for d in range(1, NX):
        @pl.when(ix + d < NX)
        def _():
            for n in range(2):
                b_copy(d, n, row0).start()

    lax.fori_loop(half, heads, local_part, 0)

    for d in range(1, NX):
        @pl.when(ix - d >= 0)
        def _():
            for n in range(2):
                b_copy(d, n, pl.multiple_of(BLOCK + (ix - d) * plane, plane)).wait_recv()

    far_keep = far_id < me

    def full_part(h, _):
        c = cols(h)
        q = qv[:, c]
        g = gv[:, c]
        ga = (g.astype(F32) * gain_ref[:, c]).astype(BF16)
        kh = kc[:, c]
        vh = vc[:, c]
        s_far = jnp.where(far_keep, dot(kc[pl.ds(BLOCK, blocks), c], q, ((1,), (1,))), neg)
        dp_far = dot(vc[pl.ds(BLOCK, blocks), c], ga, ((1,), (1,)))
        s = jnp.concatenate([st[h], s_far], axis=0)
        dprob = jnp.concatenate([dpt[h], dp_far], axis=0)
        top = jnp.max(s, axis=0, keepdims=True)
        e = jnp.exp2((s - top) * escale)
        prob = e * (1.0 / jnp.sum(e, axis=0, keepdims=True))
        row_dot = jnp.sum(prob * dprob, axis=0, keepdims=True)
        ds = (prob * (dprob - row_dot)).astype(BF16)
        ph = prob.astype(BF16)
        both = dot(ph, jnp.concatenate([g, ga], axis=1), ((1,), (0,)))
        gpart[:, c] = jnp.sum(vh.astype(F32) * both[:, :DIM], axis=0, keepdims=True)
        gval = both[:, DIM:]
        gkey = dot(ds, q, ((1,), (0,))) * scale
        gqo[:, c] = (dot(ds, kh, ((0,), (0,))) * scale).astype(BF16)
        gko[:, c] = gkey[:BLOCK].astype(BF16)
        gvo[:, c] = gval[:BLOCK].astype(BF16)
        lastk[:, c] = gkey[first:BLOCK]
        lastv[:, c] = gval[first:BLOCK]
        send[:, c] = gkey[BLOCK:].astype(BF16)
        send[:, cols(h, features)] = gval[BLOCK:].astype(BF16)
        return 0

    width = features // GROUPS

    def c_copy(d, grp, n):
        lo = pl.multiple_of(lax.rem(ix - d + NX, NX) * plane, plane)
        cc = pl.ds(n * features + grp * width, width)
        return pltpu.make_async_remote_copy(
            src_ref=send.at[pl.ds(lo, plane), cc], dst_ref=rbuf.at[d - 1, :, cc],
            send_sem=c_s.at[d - 1, grp, n], recv_sem=c_r.at[d - 1, grp, n],
            device_id={"ctx": lax.rem(ix - d + NX, NX) * plane + ip}, device_id_type=MESH)

    per = heads // GROUPS
    for grp in range(GROUPS):
        lax.fori_loop(grp * per, (grp + 1) * per, full_part, 0)
        for d in range(1, NX):
            @pl.when(ix - d >= 0)
            def _():
                for n in range(2):
                    c_copy(d, grp, n).start()

    gain_groups = (
        (NY, iy, lambda o: {"ctx": ctx_of(ix, o, iz)}),
        (NX * NZ, ix * NZ + iz, lambda o: {"ctx": ctx_of(lax.div(o, NZ), iy, lax.rem(o, NZ))}),
        (ndp, dp, lambda o: {"dp": o}),
    )

    def gain_copy(stage, j, slot):
        size, mine, where = gain_groups[stage]
        buf = (gb1, gb2, gb3)[stage]
        other = lax.rem(mine + j, size)
        s = mine if slot is None else other
        return pltpu.make_async_remote_copy(
            src_ref=buf.at[s], dst_ref=buf.at[s], send_sem=g_s.at[stage, j], recv_sem=g_r.at[stage, s],
            device_id=where(other), device_id_type=MESH)

    def gain_start(stage, value):
        size, mine, _ = gain_groups[stage]
        (gb1, gb2, gb3)[stage][mine] = value
        for j in range(1, size):
            gain_copy(stage, j, None).start()

    def gain_end(stage):
        size, _, _ = gain_groups[stage]
        for j in range(1, size):
            gain_copy(stage, j, 1).wait_recv()
        buf = (gb1, gb2, gb3)[stage]
        total = buf[0]
        for i in range(1, size):
            total = total + buf[i]
        return total

    gain_start(0, gpart[...])

    pltpu.make_async_copy(gqo, gq_hbm, outsem.at[0]).start()
    for n, (src, dst) in enumerate(((gko, gk_hbm), (gvo, gv_hbm))):
        pltpu.make_async_copy(src.at[pl.ds(0, first)], dst.at[pl.ds(0, first)], outsem.at[1 + n]).start()

    acc[...] = send[pl.ds(pl.multiple_of(ix * plane, plane), plane)].astype(F32)
    gain_start(1, gain_end(0))
    for d in range(1, NX):
        @pl.when(ix + d < NX)
        def _():
            for grp in range(GROUPS):
                for n in range(2):
                    c_copy(d, grp, n).wait_recv()
            acc[...] += rbuf[d - 1].astype(F32)

    both_rows = jnp.concatenate([acc[:, :features], acc[:, features:]], axis=0).astype(BF16)
    pairs[...] = dot(apart, both_rows, ((0,), (0,)))
    for i in range(plane):
        asend[i] = pairs[pl.ds(2 * i, 2)].astype(BF16)

    def d_copy(j, recv):
        p = lax.rem(ip + j, plane)
        return pltpu.make_async_remote_copy(
            src_ref=asend.at[p], dst_ref=arecv.at[p if recv else ip],
            send_sem=d_s.at[j], recv_sem=d_r.at[p if recv else ip],
            device_id={"ctx": ix * plane + p}, device_id_type=MESH)

    for j in range(1, plane):
        d_copy(j, False).start()
    arecv[ip] = asend[ip]
    gain_start(2, gain_end(1))
    for j in range(1, plane):
        d_copy(j, True).wait_recv()
    total = arecv[0].astype(F32)
    for i in range(1, plane):
        total = total + arecv[i].astype(F32)
    last = lax.broadcasted_iota(jnp.int32, (16, features), 0) == 15
    gko[pl.ds(first, 16)] = (lastk[...] + jnp.where(last, total[0:1], 0.0)).astype(BF16)
    gvo[pl.ds(first, 16)] = (lastv[...] + jnp.where(last, total[1:2], 0.0)).astype(BF16)
    for n, (src, dst) in enumerate(((gko, gk_hbm), (gvo, gv_hbm))):
        pltpu.make_async_copy(src.at[pl.ds(first, 16)], dst.at[pl.ds(first, 16)], outsem.at[3 + n]).start()

    gg_ref[...] = gain_end(2) * (1.0 / ndp)

    pltpu.make_async_copy(gqo, gq_hbm, outsem.at[0]).wait()
    for n, (src, dst) in enumerate(((gko, gk_hbm), (gvo, gv_hbm))):
        pltpu.make_async_copy(src.at[pl.ds(0, first)], dst.at[pl.ds(0, first)], outsem.at[1 + n]).wait()
        pltpu.make_async_copy(src.at[pl.ds(first, 16)], dst.at[pl.ds(first, 16)], outsem.at[3 + n]).wait()
    for j in range(1, plane):
        a_copy(j).wait_send()
        d_copy(j, False).wait_send()
    for d in range(1, NX):
        @pl.when(ix + d < NX)
        def _():
            for n in range(2):
                b_copy(d, n, row0).wait_send()

        @pl.when(ix - d >= 0)
        def _():
            for grp in range(GROUPS):
                for n in range(2):
                    c_copy(d, grp, n).wait_send()
    for stage in range(3):
        for j in range(1, gain_groups[stage][0]):
            gain_copy(stage, j, None).wait_send()


def body(ndp, query_proj, key_proj, value_proj, out_grad, out_gain):
    features = query_proj.shape[2]
    heads = features // DIM
    plane = NY * NZ
    blocks = NX * plane
    flat = lambda a: a.reshape(BLOCK, features)
    any_spec = pl.BlockSpec(memory_space=pl.ANY)
    vmem_spec = pl.BlockSpec(memory_space=pltpu.VMEM)
    dma = pltpu.SemaphoreType.DMA
    rows = jax.ShapeDtypeStruct((BLOCK, features), BF16)
    outs = pl.pallas_call(
        functools.partial(kernel, heads, ndp),
        out_shape=(rows, rows, rows, jax.ShapeDtypeStruct((1, features), F32)),
        in_specs=[any_spec] * 4 + [vmem_spec],
        out_specs=(any_spec, any_spec, any_spec, vmem_spec),
        scratch_shapes=[
            pltpu.VMEM((BLOCK, features), BF16),
            pltpu.VMEM((BLOCK + blocks, features), BF16),
            pltpu.VMEM((BLOCK + blocks, features), BF16),
            pltpu.VMEM((BLOCK, features), BF16),
            pltpu.VMEM((BLOCK, features), BF16),
            pltpu.VMEM((BLOCK, features), BF16),
            pltpu.VMEM((BLOCK, features), BF16),
            pltpu.VMEM((16, features), F32),
            pltpu.VMEM((16, features), F32),
            pltpu.VMEM((heads, BLOCK, BLOCK), F32),
            pltpu.VMEM((heads, BLOCK, BLOCK), F32),
            pltpu.VMEM((plane, 2, features), BF16),
            pltpu.VMEM((blocks, 2 * features), BF16),
            pltpu.VMEM((NX - 1, plane, 2 * features), BF16),
            pltpu.VMEM((plane, 2 * features), F32),
            pltpu.VMEM((2 * plane, features), F32),
            pltpu.VMEM((plane, 2, features), BF16),
            pltpu.VMEM((plane, 2, features), BF16),
            pltpu.VMEM((1, features), F32),
            pltpu.VMEM((NY, 1, features), F32),
            pltpu.VMEM((NX * NZ, 1, features), F32),
            pltpu.VMEM((ndp, 1, features), F32),
            dma((6,)),
            dma((5,)),
            dma((plane,)),
            dma((plane,)),
            dma((NX, 2)),
            dma((NX, 2)),
            dma((NX - 1, GROUPS, 2)),
            dma((NX - 1, GROUPS, 2)),
            dma((plane,)),
            dma((plane,)),
            dma((3, max(NY, NX * NZ, ndp))),
            dma((3, max(NY, NX * NZ, ndp))),
        ],
        compiler_params=pltpu.CompilerParams(
            collective_id=0, has_side_effects=True, vmem_limit_bytes=56 * 1024 * 1024
        ),
    )(flat(query_proj), flat(key_proj), flat(value_proj), flat(out_grad), out_gain.reshape(1, features))
    shape = (1, BLOCK, features)
    return (outs[0].reshape(shape), outs[1].reshape(shape), outs[2].reshape(shape), outs[3].reshape(features))


def solution(mesh):
    spec = P("dp", "ctx", None)
    return jax.shard_map(
        functools.partial(body, mesh.shape["dp"]),
        mesh=mesh,
        in_specs=(spec, spec, spec, spec, P()),
        out_specs=(spec, spec, spec, P()),
        check_vma=False,
    )
```

```python
import functools
import math

import jax
import jax.numpy as jnp
from jax import lax
from jax.experimental import pallas as pl
from jax.experimental.pallas import tpu as pltpu
from jax.sharding import PartitionSpec as P

DIM = 128
BLOCK = 128
NX, NY, NZ = 4, 8, 2
CHUNKS = 4
MESH = pl.DeviceIdType.MESH
F32 = jnp.float32
BF16 = jnp.bfloat16


def dot(a, b, dims):
    return lax.dot_general(a, b, (dims, ((), ())), preferred_element_type=F32)


def kernel(
    heads, ndp,
    q_hbm, k_hbm, v_hbm, g_hbm, gain_hbm,
    gqo, gko, gvo, gg_ref,
    qv, kc, vc, gv, gav, gain_ref, lastk, lastv, st, dpt,
    gvf, tails, panel, send, rbuf, acc, pairs, dsend, drecv, gpart, gb1, gb2, gb3,
    insem, a_s, a_r, b_s, b_r, c_s, c_r, d_s, d_r, g_s, g_r,
):
    features = heads * DIM
    nb = NX * NZ
    blocks = NX * NY * NZ
    per = heads // CHUNKS
    width = per * DIM
    scale = 1.0 / math.sqrt(DIM)
    escale = scale * math.log2(math.e)
    dp = lax.axis_index("dp")
    me = lax.axis_index("ctx")
    ix = lax.div(me, NY * NZ)
    iy = lax.rem(lax.div(me, NZ), NY)
    iz = lax.rem(me, NZ)
    ib = ix * NZ + iz

    def y_peer(o):
        return {"ctx": (ix * NY + o) * NZ + iz}

    def b_peer(o):
        return {"ctx": (lax.div(o, NZ) * NY + iy) * NZ + lax.rem(o, NZ)}

    def dp_peer(o):
        return {"dp": o}

    first = BLOCK - 16
    loads = []

    def load(n, src, dst):
        cp = pltpu.make_async_copy(src, dst, insem.at[n])
        cp.start()
        loads.append(cp)

    load(0, k_hbm.at[pl.ds(first, 16)], kc.at[pl.ds(first, 16)])
    load(1, v_hbm.at[pl.ds(first, 16)], vc.at[pl.ds(first, 16)])
    load(2, k_hbm.at[pl.ds(0, first)], kc.at[pl.ds(0, first)])
    load(3, q_hbm, qv)
    load(4, v_hbm.at[pl.ds(0, first)], vc.at[pl.ds(0, first)])
    load(5, g_hbm, gv)
    load(6, gain_hbm, gain_ref)

    panel[...] = jnp.zeros_like(panel)

    barrier = pltpu.get_barrier_semaphore()

    def greet(device):
        pl.semaphore_signal(barrier, inc=1, device_id=device, device_id_type=MESH)

    for j in range(1, NY):
        greet(y_peer(lax.rem(iy + j, NY)))
    for j in range(1, nb):
        greet(b_peer(lax.rem(ib + j, nb)))
    for j in range(1, ndp):
        greet(dp_peer(lax.rem(dp + j, ndp)))

    loads[0].wait()
    loads[1].wait()
    ktail = kc[pl.ds(first, 16)].astype(F32)[15:16]
    vtail = vc[pl.ds(first, 16)].astype(F32)[15:16]
    tails[iy] = jnp.concatenate([ktail, vtail], axis=0).astype(BF16)

    pl.semaphore_wait(barrier, NY + nb + ndp - 3)

    def a_copy(j, recv):
        p = lax.rem(iy + j, NY)
        s = p if recv else iy
        return pltpu.make_async_remote_copy(
            src_ref=tails.at[s], dst_ref=tails.at[s], send_sem=a_s.at[j], recv_sem=a_r.at[s],
            device_id=y_peer(p), device_id_type=MESH)

    for j in range(1, NY):
        a_copy(j, False).start()

    key_id = lax.broadcasted_iota(jnp.int32, (BLOCK, BLOCK), 0)
    query_id = lax.broadcasted_iota(jnp.int32, (BLOCK, BLOCK), 1)
    neg = -jnp.inf

    def cols(h):
        return pl.ds(pl.multiple_of(h * DIM, DIM), DIM)

    def local_scores(h, _):
        c = cols(h)
        s = dot(kc[pl.ds(0, BLOCK), c], qv[:, c], ((1,), (1,)))
        st[h, pl.ds(0, BLOCK)] = jnp.where(key_id <= query_id, s, neg)
        return 0

    def local_dprob(h, _):
        c = cols(h)
        ga = (gv[:, c].astype(F32) * gain_ref[pl.ds(h, 1), :]).astype(BF16)
        gav[:, c] = ga
        dpt[h] = dot(vc[pl.ds(0, BLOCK), c], ga, ((1,), (1,)))
        return 0

    loads[2].wait()
    loads[3].wait()
    lax.fori_loop(0, heads, local_scores, 0, unroll=per)
    loads[4].wait()
    loads[5].wait()
    loads[6].wait()
    lax.fori_loop(0, heads, local_dprob, 0, unroll=per)

    for j in range(1, NY):
        a_copy(j, True).wait_recv()
    for i in range(NY):
        pairs[pl.ds(2 * i, 2)] = tails[i].astype(F32)
    to_id = lax.broadcasted_iota(jnp.int32, (2 * NY, 2 * NY), 0)
    from_id = lax.broadcasted_iota(jnp.int32, (2 * NY, 2 * NY), 1)
    apart = jnp.where(from_id == 2 * lax.rem(to_id, NY) + lax.div(to_id, NY), 1.0, 0.0).astype(BF16)
    panel[ib] = dot(apart, pairs[...].astype(BF16), ((1,), (0,))).astype(BF16)

    def chunk(c):
        return pl.ds(c * width, width)

    def b_copy(c, j, recv):
        p = lax.rem(ib + j, nb)
        s = p if recv else ib
        return pltpu.make_async_remote_copy(
            src_ref=panel.at[s, :, chunk(c)], dst_ref=panel.at[s, :, chunk(c)],
            send_sem=b_s.at[c, j], recv_sem=b_r.at[c, s],
            device_id=b_peer(p), device_id_type=MESH)

    def later(j):
        return lax.div(lax.rem(ib + j, nb), NZ) >= ix

    def earlier(j):
        return lax.div(lax.rem(ib + j, nb), NZ) <= ix

    for c in range(CHUNKS):
        for j in range(1, nb):
            @pl.when(later(j))
            def _():
                b_copy(c, j, False).start()

    row = lax.broadcasted_iota(jnp.int32, (blocks, BLOCK), 0)
    far_id = (lax.div(row, NY * NZ) * NY + lax.rem(row, NY)) * NZ + lax.rem(lax.div(row, NY), NZ)
    far_keep = far_id < me
    far = pl.ds(BLOCK, blocks)

    def forward(h, _):
        c = cols(h)
        s_far = jnp.where(far_keep, dot(kc[far, c], qv[:, c], ((1,), (1,))), neg)
        s = jnp.concatenate([st[h, pl.ds(0, BLOCK)], s_far], axis=0)
        top = jnp.max(s, axis=0, keepdims=True)
        e = jnp.exp2((s - top) * escale)
        prob = e * (1.0 / jnp.sum(e, axis=0, keepdims=True))
        st[h] = prob
        both = dot(prob.astype(BF16), jnp.concatenate([gv[:, c], gav[:, c]], axis=1), ((1,), (0,)))
        gpart[pl.ds(h, 1), :] = jnp.sum(vc[:, c].astype(F32) * both[:, :DIM], axis=0, keepdims=True)
        gval = both[:, DIM:]
        gvo[:, c] = gval[:BLOCK].astype(BF16)
        lastv[:, c] = gval[first:BLOCK]
        gvf[:, c] = gval[BLOCK:]
        return 0

    def backward(h, _):
        c = cols(h)
        prob = st[h]
        dprob = jnp.concatenate([dpt[h], dot(vc[far, c], gav[:, c], ((1,), (1,)))], axis=0)
        row_dot = jnp.sum(prob * dprob, axis=0, keepdims=True)
        ds = (prob * (dprob - row_dot)).astype(BF16)
        gkey = dot(ds, qv[:, c], ((1,), (0,))) * scale
        gqo[:, c] = (dot(ds, kc[:, c], ((0,), (0,))) * scale).astype(BF16)
        gko[:, c] = gkey[:BLOCK].astype(BF16)
        lastk[:, c] = gkey[first:BLOCK]
        for i in range(nb):
            at = slice(BLOCK + i * NY, BLOCK + (i + 1) * NY)
            send[i, :, c] = jnp.concatenate([gkey[at], gvf[pl.ds(i * NY, NY), c]], axis=0).astype(BF16)
        return 0

    def c_copy(c, j, recv):
        p = lax.rem(ib + j, nb)
        s = p if recv else ib
        return pltpu.make_async_remote_copy(
            src_ref=send.at[p, :, chunk(c)], dst_ref=rbuf.at[s, :, chunk(c)],
            send_sem=c_s.at[c, j], recv_sem=c_r.at[c, s],
            device_id=b_peer(p), device_id_type=MESH)

    gain_groups = ((NY, iy, y_peer, gb1), (nb, ib, b_peer, gb2), (ndp, dp, dp_peer, gb3))

    def gain_copy(stage, j, recv):
        size, mine, where, buf = gain_groups[stage]
        p = lax.rem(mine + j, size)
        s = p if recv else mine
        return pltpu.make_async_remote_copy(
            src_ref=buf.at[s], dst_ref=buf.at[s], send_sem=g_s.at[stage, j], recv_sem=g_r.at[stage, s],
            device_id=where(p), device_id_type=MESH)

    def gain_start(stage, value):
        size, mine, _, buf = gain_groups[stage]
        buf[mine] = value
        for j in range(1, size):
            gain_copy(stage, j, False).start()

    def gain_end(stage):
        size, _, _, buf = gain_groups[stage]
        for j in range(1, size):
            gain_copy(stage, j, True).wait_recv()
        total = buf[0]
        for i in range(1, size):
            total = total + buf[i]
        return total

    for c in range(CHUNKS):
        for j in range(1, nb):
            @pl.when(earlier(j))
            def _():
                b_copy(c, j, True).wait_recv()
        for i in range(0, nb, 2):
            one = panel[i, :, chunk(c)].astype(F32)
            two = panel[i + 1, :, chunk(c)].astype(F32)
            at = pl.ds(BLOCK + i * NY, 2 * NY)
            kc[at, chunk(c)] = jnp.concatenate([one[:NY], two[:NY]], axis=0).astype(BF16)
            vc[at, chunk(c)] = jnp.concatenate([one[NY:], two[NY:]], axis=0).astype(BF16)
        lax.fori_loop(c * per, (c + 1) * per, forward, 0, unroll=per)
        if c == CHUNKS - 1:
            gain_start(0, gpart[...])
        lax.fori_loop(c * per, (c + 1) * per, backward, 0, unroll=per)
        for j in range(1, nb):
            @pl.when(earlier(j))
            def _():
                c_copy(c, j, False).start()

    def d_copy(grp, j, recv):
        lo, hi = grp
        p = lax.rem(iy + j, NY)
        cc = pl.ds(lo * width, (hi - lo) * width)
        return pltpu.make_async_remote_copy(
            src_ref=dsend.at[p, :, cc], dst_ref=drecv.at[p if recv else iy, :, cc],
            send_sem=d_s.at[lo, j], recv_sem=d_r.at[lo, p if recv else iy],
            device_id=y_peer(p), device_id_type=MESH)

    def owners(grp):
        lo, hi = grp
        cc = pl.ds(lo * width, (hi - lo) * width)
        acc[:, cc] = send[ib, :, cc].astype(F32)
        for j in range(1, nb):
            @pl.when(later(j))
            def _():
                for c in range(lo, hi):
                    c_copy(c, j, True).wait_recv()
                acc[:, cc] += rbuf[lax.rem(ib + j, nb), :, cc].astype(F32)
        pairs[:, cc] = dot(apart, acc[:, cc].astype(BF16), ((0,), (0,)))
        for i in range(NY):
            dsend[i, :, cc] = pairs[pl.ds(2 * i, 2), cc].astype(BF16)
        for j in range(1, NY):
            d_copy(grp, j, False).start()
        drecv[iy, :, cc] = dsend[iy, :, cc]

    groups = ((0, CHUNKS - 1), (CHUNKS - 1, CHUNKS))
    owners(groups[0])
    gain_start(1, gain_end(0))
    owners(groups[1])
    gain_start(2, gain_end(1))
    for grp in groups:
        for j in range(1, NY):
            d_copy(grp, j, True).wait_recv()
    total = drecv[0].astype(F32)
    for i in range(1, NY):
        total = total + drecv[i].astype(F32)
    last = lax.broadcasted_iota(jnp.int32, (16, features), 0) == 15
    gko[pl.ds(first, 16)] = (lastk[...] + jnp.where(last, total[0:1], 0.0)).astype(BF16)
    gvo[pl.ds(first, 16)] = (lastv[...] + jnp.where(last, total[1:2], 0.0)).astype(BF16)

    gg_ref[...] = gain_end(2) * (1.0 / ndp)

    for j in range(1, NY):
        a_copy(j, False).wait_send()
        for grp in groups:
            d_copy(grp, j, False).wait_send()
    for j in range(1, nb):
        @pl.when(later(j))
        def _():
            for c in range(CHUNKS):
                b_copy(c, j, False).wait_send()

        @pl.when(earlier(j))
        def _():
            for c in range(CHUNKS):
                c_copy(c, j, False).wait_send()
    for stage in range(3):
        for j in range(1, gain_groups[stage][0]):
            gain_copy(stage, j, False).wait_send()


def write_out(a, b, c, d, a_hbm, b_hbm, c_hbm, d_hbm, sem):
    copies = [
        pltpu.make_async_copy(src, dst, sem.at[n])
        for n, (src, dst) in enumerate(((a, a_hbm), (b, b_hbm), (c, c_hbm), (d, d_hbm)))
    ]
    for cp in copies:
        cp.start()
    for cp in copies:
        cp.wait()


def body(ndp, query_proj, key_proj, value_proj, out_grad, out_gain):
    features = query_proj.shape[2]
    heads = features // DIM
    nb = NX * NZ
    blocks = NX * NY * NZ
    flat = lambda a: a.reshape(BLOCK, features)
    hbm = pl.BlockSpec(memory_space=pltpu.HBM)
    vmem = pl.BlockSpec(memory_space=pltpu.VMEM)
    dma = pltpu.SemaphoreType.DMA
    most = max(NY, nb, ndp)
    outs = pl.pallas_call(
        functools.partial(kernel, heads, ndp),
        out_shape=(
            pltpu.VMEM((BLOCK, features), BF16),
            pltpu.VMEM((BLOCK, features), BF16),
            pltpu.VMEM((BLOCK, features), BF16),
            pltpu.VMEM((heads, DIM), F32),
        ),
        in_specs=[hbm] * 5,
        out_specs=(vmem,) * 4,
        scratch_shapes=[
            pltpu.VMEM((BLOCK, features), BF16),
            pltpu.VMEM((BLOCK + blocks, features), BF16),
            pltpu.VMEM((BLOCK + blocks, features), BF16),
            pltpu.VMEM((BLOCK, features), BF16),
            pltpu.VMEM((BLOCK, features), BF16),
            pltpu.VMEM((heads, DIM), F32),
            pltpu.VMEM((16, features), F32),
            pltpu.VMEM((16, features), F32),
            pltpu.VMEM((heads, BLOCK + blocks, BLOCK), F32),
            pltpu.VMEM((heads, BLOCK, BLOCK), F32),
            pltpu.VMEM((blocks, features), F32),
            pltpu.VMEM((NY, 2, features), BF16),
            pltpu.VMEM((nb, 2 * NY, features), BF16),
            pltpu.VMEM((nb, 2 * NY, features), BF16),
            pltpu.VMEM((nb, 2 * NY, features), BF16),
            pltpu.VMEM((2 * NY, features), F32),
            pltpu.VMEM((2 * NY, features), F32),
            pltpu.VMEM((NY, 2, features), BF16),
            pltpu.VMEM((NY, 2, features), BF16),
            pltpu.VMEM((heads, DIM), F32),
            pltpu.VMEM((NY, heads, DIM), F32),
            pltpu.VMEM((nb, heads, DIM), F32),
            pltpu.VMEM((ndp, heads, DIM), F32),
            dma((7,)),
            dma((NY,)),
            dma((NY,)),
            dma((CHUNKS, nb)),
            dma((CHUNKS, nb)),
            dma((CHUNKS, nb)),
            dma((CHUNKS, nb)),
            dma((CHUNKS, NY)),
            dma((CHUNKS, NY)),
            dma((3, most)),
            dma((3, most)),
        ],
        compiler_params=pltpu.CompilerParams(
            collective_id=0, has_side_effects=True, vmem_limit_bytes=52 * 1024 * 1024
        ),
    )(flat(query_proj), flat(key_proj), flat(value_proj), flat(out_grad), out_gain.reshape(heads, DIM))
    rows = jax.ShapeDtypeStruct((BLOCK, features), BF16)
    outs = pl.pallas_call(
        write_out,
        out_shape=(rows, rows, rows, jax.ShapeDtypeStruct((heads, DIM), F32)),
        in_specs=[vmem] * 4,
        out_specs=(hbm,) * 4,
        scratch_shapes=[dma((4,))],
        compiler_params=pltpu.CompilerParams(vmem_limit_bytes=2 * 1024 * 1024),
    )(*outs)
    shape = (1, BLOCK, features)
    return (outs[0].reshape(shape), outs[1].reshape(shape), outs[2].reshape(shape), outs[3].reshape(features))


def solution(mesh):
    spec = P("dp", "ctx", None)
    return jax.shard_map(
        functools.partial(body, mesh.shape["dp"]),
        mesh=mesh,
        in_specs=(spec, spec, spec, spec, P()),
        out_specs=(spec, spec, spec, P()),
        check_vma=False,
    )
```

```python
import functools
import math

import jax
import jax.numpy as jnp
from jax import lax
from jax.experimental import pallas as pl
from jax.experimental.pallas import tpu as pltpu
from jax.sharding import PartitionSpec as P

DIM = 128
BLOCK = 128
NX, NY, NZ = 4, 8, 2
CHUNKS = 2
PAD = 8
MESH = pl.DeviceIdType.MESH
F32 = jnp.float32
BF16 = jnp.bfloat16


def y_order():
    return sorted(range(NY), key=lambda o: (min(o, NY - o), o))


def waves():
    ends = [0, 1, min(5, NY), NY]
    return [(a, b) for a, b in zip(ends, ends[1:]) if a < b]


def dot(a, b, dims):
    return lax.dot_general(a, b, (dims, ((), ())), preferred_element_type=F32)


def kernel(
    heads, ndp,
    q_hbm, k_hbm, v_hbm, g_hbm, gain_hbm,
    gqo, gko, gvo, gg_ref,
    qv, kc, vc, gv, gav, gain_ref, lastk, lastv, st, dpt,
    gvf, panel, mixed, send, rbuf, acc, pairs, dsend, drecv, gpart, gb1, gb2, gb3,
    insem, a_s, a_r, b_s, b_r, c_s, c_r, d_s, d_r, g_s, g_r,
):
    features = heads * DIM
    nb = NX * NZ
    blocks = NX * NY * NZ
    per = heads // CHUNKS
    width = per * DIM
    scale = 1.0 / math.sqrt(DIM)
    escale = scale * math.log2(math.e)
    dp = lax.axis_index("dp")
    me = lax.axis_index("ctx")
    ix = lax.div(me, NY * NZ)
    iy = lax.rem(lax.div(me, NZ), NY)
    iz = lax.rem(me, NZ)
    ib = ix * NZ + iz
    order = y_order()
    slot_of = [order.index(o) for o in range(NY)]

    def y_peer(o):
        return {"ctx": (ix * NY + o) * NZ + iz}

    def b_peer(o):
        return {"ctx": (lax.div(o, NZ) * NY + iy) * NZ + lax.rem(o, NZ)}

    def dp_peer(o):
        return {"dp": o}

    first = BLOCK - 16
    loads = []

    def load(n, src, dst):
        cp = pltpu.make_async_copy(src, dst, insem.at[n])
        cp.start()
        loads.append(cp)

    load(0, k_hbm.at[pl.ds(first, 16)], kc.at[pl.ds(first, 16)])
    load(1, v_hbm.at[pl.ds(first, 16)], vc.at[pl.ds(first, 16)])
    load(2, k_hbm.at[pl.ds(0, first)], kc.at[pl.ds(0, first)])
    load(3, q_hbm, qv)
    load(4, v_hbm.at[pl.ds(0, first)], vc.at[pl.ds(0, first)])
    load(5, g_hbm, gv)
    load(6, gain_hbm, gain_ref)

    barrier = pltpu.get_barrier_semaphore()

    def greet(device):
        pl.semaphore_signal(barrier, inc=1, device_id=device, device_id_type=MESH)

    for j in range(1, NY):
        greet(y_peer(lax.rem(iy + j, NY)))
    for j in range(1, nb):
        greet(b_peer(lax.rem(ib + j, nb)))
    for j in range(1, ndp):
        greet(dp_peer(lax.rem(dp + j, ndp)))

    loads[0].wait()
    loads[1].wait()
    ktail = kc[pl.ds(first, 16)].astype(F32)[15:16]
    vtail = vc[pl.ds(first, 16)].astype(F32)[15:16]
    panel[ib, 0] = jnp.concatenate([ktail, vtail], axis=0).astype(BF16)
    gpart[...] = jnp.zeros_like(gpart)

    pl.semaphore_wait(barrier, NY + nb + ndp - 3)

    def a_copy(j, recv):
        p = lax.rem(iy + j, NY)
        s = slot_of[j if recv else NY - j]
        return pltpu.make_async_remote_copy(
            src_ref=panel.at[ib, 0], dst_ref=panel.at[ib, s], send_sem=a_s.at[j], recv_sem=a_r.at[s],
            device_id=y_peer(p), device_id_type=MESH)

    def later(j):
        return lax.div(lax.rem(ib + j, nb), NZ) >= ix

    def earlier(j):
        return lax.div(lax.rem(ib + j, nb), NZ) <= ix

    pieces = [(0, 1, 0, features)]
    for c in range(CHUNKS):
        for lo, hi in waves()[1:]:
            pieces.append((lo, hi, c * width, width))
    per_chunk = len(waves()) - 1

    def b_copy(n, j, recv):
        lo, hi, start, size = pieces[n]
        p = lax.rem(ib + j, nb)
        s = p if recv else ib
        part = (s, pl.ds(lo, hi - lo), slice(None), pl.ds(start, size))
        return pltpu.make_async_remote_copy(
            src_ref=panel.at[part], dst_ref=panel.at[part],
            send_sem=b_s.at[n, j], recv_sem=b_r.at[n, s],
            device_id=b_peer(p), device_id_type=MESH)

    def send_on(n):
        for j in range(1, nb):
            @pl.when(later(j))
            def _():
                b_copy(n, j, False).start()

    def wave_here(n):
        for s in range(max(1, waves()[n][0]), waves()[n][1]):
            a_copy(order[s], True).wait_recv()

    for j in order[:0:-1]:
        a_copy(j, False).start()
    send_on(0)

    for j in range(1, nb):
        @pl.when(jnp.logical_not(earlier(j)))
        def _():
            panel[lax.rem(ib + j, nb)] = jnp.zeros(panel.shape[1:], BF16)

    key_id = lax.broadcasted_iota(jnp.int32, (BLOCK, BLOCK), 0)
    query_id = lax.broadcasted_iota(jnp.int32, (BLOCK, BLOCK), 1)
    neg = -jnp.inf

    def cols(h):
        return pl.ds(pl.multiple_of(h * DIM, DIM), DIM)

    def local_scores(h, _):
        c = cols(h)
        s = dot(kc[pl.ds(0, BLOCK), c], qv[:, c], ((1,), (1,)))
        st[h, pl.ds(0, BLOCK)] = jnp.where(key_id <= query_id, s, neg)
        return 0

    def local_dprob(h, _):
        c = cols(h)
        ga = (gv[:, c].astype(F32) * gain_ref[pl.ds(h, 1), :]).astype(BF16)
        gav[:, c] = ga
        dpt[h] = dot(vc[pl.ds(0, BLOCK), c], ga, ((1,), (1,)))
        return 0

    loads[2].wait()
    loads[3].wait()
    lax.fori_loop(0, heads, local_scores, 0, unroll=5)
    wave_here(1)
    send_on(1)
    loads[4].wait()
    loads[5].wait()
    loads[6].wait()
    lax.fori_loop(0, heads, local_dprob, 0, unroll=5)

    for n in range(2, len(waves())):
        wave_here(n)
    for n in range(2, len(pieces)):
        send_on(n)

    def sorter(n):
        to_id = lax.broadcasted_iota(jnp.int32, (2 * n, 2 * n), 0)
        from_id = lax.broadcasted_iota(jnp.int32, (2 * n, 2 * n), 1)
        return jnp.where(from_id == 2 * lax.rem(to_id, n) + lax.div(to_id, n), 1.0, 0.0).astype(BF16)

    def chunk(c):
        return pl.ds(c * width, width)

    row = lax.broadcasted_iota(jnp.int32, (blocks, BLOCK), 0)
    off = jnp.zeros_like(row)
    for i in range(1, NY):
        off = jnp.where(lax.rem(row, NY) == i, order[i], off)
    far_id = (lax.div(row, NY * NZ) * NY + lax.rem(iy + off, NY)) * NZ + lax.rem(lax.div(row, NY), NZ)
    far_keep = far_id < me
    far = pl.ds(BLOCK, blocks)

    def fwd(h):
        c = cols(h)
        s_far = jnp.where(far_keep, dot(kc[far, c], qv[:, c], ((1,), (1,))), neg)
        s = jnp.concatenate([st[h, pl.ds(0, BLOCK)], s_far], axis=0)
        top = jnp.max(s, axis=0, keepdims=True)
        e = jnp.exp2((s - top) * escale)
        prob = e * (1.0 / jnp.sum(e, axis=0, keepdims=True))
        both = dot(prob.astype(BF16), jnp.concatenate([gv[:, c], gav[:, c]], axis=1), ((1,), (0,)))
        gpart[pl.ds(h, 1), :] = jnp.sum(vc[:, c].astype(F32) * both[:, :DIM], axis=0, keepdims=True)
        gval = both[:, DIM:]
        gvo[:, c] = gval[:BLOCK].astype(BF16)
        lastv[:, c] = gval[first:BLOCK]
        gvf[:, c] = gval[BLOCK:]
        return prob

    def bwd(h, prob):
        c = cols(h)
        dprob = jnp.concatenate([dpt[h], dot(vc[far, c], gav[:, c], ((1,), (1,)))], axis=0)
        row_dot = jnp.sum(prob * dprob, axis=0, keepdims=True)
        ds = (prob * (dprob - row_dot)).astype(BF16)
        gkey = dot(ds, qv[:, c], ((1,), (0,))) * scale
        gqo[:, c] = (dot(ds, kc[:, c], ((0,), (0,))) * scale).astype(BF16)
        gko[:, c] = gkey[:BLOCK].astype(BF16)
        lastk[:, c] = gkey[first:BLOCK]
        for i in range(nb):
            at = slice(BLOCK + i * NY, BLOCK + (i + 1) * NY)
            send[i, :, c] = jnp.concatenate([gkey[at], gvf[pl.ds(i * NY, NY), c]], axis=0).astype(BF16)

    def forward(h, _):
        st[h] = fwd(h)
        return 0

    def backward(h, _):
        bwd(h, st[h])
        return 0

    def whole(h, _):
        bwd(h, fwd(h))
        return 0

    def c_copy(c, j, recv):
        p = lax.rem(ib + j, nb)
        s = p if recv else ib
        return pltpu.make_async_remote_copy(
            src_ref=send.at[p, :, chunk(c)], dst_ref=rbuf.at[s, :, chunk(c)],
            send_sem=c_s.at[c, j], recv_sem=c_r.at[c, s],
            device_id=b_peer(p), device_id_type=MESH)

    gain_groups = ((NY, iy, y_peer, gb1), (nb, ib, b_peer, gb2), (ndp, dp, dp_peer, gb3))

    def gain_copy(stage, j, recv):
        size, mine, where, buf = gain_groups[stage]
        p = lax.rem(mine + j, size)
        s = p if recv else mine
        return pltpu.make_async_remote_copy(
            src_ref=buf.at[s], dst_ref=buf.at[s], send_sem=g_s.at[stage, j], recv_sem=g_r.at[stage, s],
            device_id=where(p), device_id_type=MESH)

    def gain_start(stage, value):
        size, mine, _, buf = gain_groups[stage]
        for t in range(value.shape[0] // PAD):
            buf[mine, t] = value[t * PAD : (t + 1) * PAD].astype(BF16)
        for j in range(1, size):
            gain_copy(stage, j, False).start()

    def gain_end(stage):
        size, _, _, buf = gain_groups[stage]
        for j in range(1, size):
            gain_copy(stage, j, True).wait_recv()
        total = []
        for t in range(buf.shape[1]):
            part = buf[0, t].astype(F32)
            for i in range(1, size):
                part = part + buf[i, t].astype(F32)
            total.append(part)
        return jnp.concatenate(total, axis=0)

    for c in range(CHUNKS):
        for j in range(1, nb):
            @pl.when(earlier(j))
            def _():
                for n in [0] * (c == 0) + [1 + c * per_chunk + w for w in range(per_chunk)]:
                    b_copy(n, j, True).wait_recv()
        rows = dot(sorter(blocks), panel[:, :, :, chunk(c)].reshape(2 * blocks, width), ((1,), (0,))).astype(BF16)
        kc[far, chunk(c)] = rows[:blocks]
        vc[far, chunk(c)] = rows[blocks:]
        ours = (c * per, (c + 1) * per)
        if c < CHUNKS - 1:
            lax.fori_loop(*ours, whole, 0, unroll=per)
        else:
            lax.fori_loop(*ours, forward, 0, unroll=per)
            gain_start(0, gpart[...])
            lax.fori_loop(*ours, backward, 0, unroll=per)
        for j in range(1, nb):
            @pl.when(earlier(j))
            def _():
                c_copy(c, j, False).start()

    def d_copy(grp, i, recv):
        lo, hi = grp
        p = lax.rem(iy + order[i], NY)
        t = i if recv else slot_of[(NY - order[i]) % NY]
        cc = pl.ds(lo * width, (hi - lo) * width)
        return pltpu.make_async_remote_copy(
            src_ref=dsend.at[i, :, cc], dst_ref=drecv.at[t, :, cc],
            send_sem=d_s.at[lo, i], recv_sem=d_r.at[lo, t],
            device_id=y_peer(p), device_id_type=MESH)

    def owners(grp):
        lo, hi = grp
        cc = pl.ds(lo * width, (hi - lo) * width)
        acc[:, cc] = send[ib, :, cc].astype(F32)
        for j in range(1, nb):
            @pl.when(later(j))
            def _():
                for c in range(lo, hi):
                    c_copy(c, j, True).wait_recv()
                acc[:, cc] += rbuf[lax.rem(ib + j, nb), :, cc].astype(F32)
        pairs[:, cc] = dot(sorter(NY), acc[:, cc].astype(BF16), ((0,), (0,)))
        for i in range(NY):
            dsend[i, :, cc] = pairs[pl.ds(2 * i, 2), cc].astype(BF16)
        for j in range(1, NY):
            d_copy(grp, j, False).start()
        drecv[0, :, cc] = dsend[0, :, cc]

    groups = ((0, CHUNKS - 1), (CHUNKS - 1, CHUNKS)) if CHUNKS > 1 else ((0, 1),)
    owners(groups[0])
    gain_start(1, gain_end(0))
    if len(groups) > 1:
        owners(groups[1])
    gain_start(2, gain_end(1))
    for grp in groups:
        for j in range(1, NY):
            d_copy(grp, j, True).wait_recv()
    total = drecv[0].astype(F32)
    for i in range(1, NY):
        total = total + drecv[i].astype(F32)
    last = lax.broadcasted_iota(jnp.int32, (16, features), 0) == 15
    gko[pl.ds(first, 16)] = (lastk[...] + jnp.where(last, total[0:1], 0.0)).astype(BF16)
    gvo[pl.ds(first, 16)] = (lastv[...] + jnp.where(last, total[1:2], 0.0)).astype(BF16)

    gg_ref[...] = gain_end(2)[:heads] * (1.0 / ndp)

    for j in range(1, NY):
        a_copy(j, False).wait_send()
        for grp in groups:
            d_copy(grp, j, False).wait_send()
    for j in range(1, nb):
        @pl.when(later(j))
        def _():
            for n in range(len(pieces)):
                b_copy(n, j, False).wait_send()

        @pl.when(earlier(j))
        def _():
            for c in range(CHUNKS):
                c_copy(c, j, False).wait_send()
    for stage in range(3):
        for j in range(1, gain_groups[stage][0]):
            gain_copy(stage, j, False).wait_send()


def write_out(a, b, c, d, a_hbm, b_hbm, c_hbm, d_hbm, sem):
    copies = [
        pltpu.make_async_copy(src, dst, sem.at[n])
        for n, (src, dst) in enumerate(((a, a_hbm), (b, b_hbm), (c, c_hbm), (d, d_hbm)))
    ]
    for cp in copies:
        cp.start()
    for cp in copies:
        cp.wait()


def body(ndp, query_proj, key_proj, value_proj, out_grad, out_gain):
    features = query_proj.shape[2]
    heads = features // DIM
    nb = NX * NZ
    blocks = NX * NY * NZ
    flat = lambda a: a.reshape(BLOCK, features)
    hbm = pl.BlockSpec(memory_space=pltpu.HBM)
    vmem = pl.BlockSpec(memory_space=pltpu.VMEM)
    dma = pltpu.SemaphoreType.DMA
    most = max(NY, nb, ndp)
    tiles = -(-heads // PAD)
    n_pieces = 1 + (len(waves()) - 1) * CHUNKS
    outs = pl.pallas_call(
        functools.partial(kernel, heads, ndp),
        out_shape=(
            pltpu.VMEM((BLOCK, features), BF16),
            pltpu.VMEM((BLOCK, features), BF16),
            pltpu.VMEM((BLOCK, features), BF16),
            pltpu.VMEM((heads, DIM), F32),
        ),
        in_specs=[hbm] * 5,
        out_specs=(vmem,) * 4,
        scratch_shapes=[
            pltpu.VMEM((BLOCK, features), BF16),
            pltpu.VMEM((BLOCK + blocks, features), BF16),
            pltpu.VMEM((BLOCK + blocks, features), BF16),
            pltpu.VMEM((BLOCK, features), BF16),
            pltpu.VMEM((BLOCK, features), BF16),
            pltpu.VMEM((heads, DIM), F32),
            pltpu.VMEM((16, features), F32),
            pltpu.VMEM((16, features), F32),
            pltpu.VMEM((heads, BLOCK + blocks, BLOCK), F32),
            pltpu.VMEM((heads, BLOCK, BLOCK), F32),
            pltpu.VMEM((blocks, features), F32),
            pltpu.VMEM((nb, NY, 2, features), BF16),
            pltpu.VMEM((2 * blocks, features // CHUNKS), F32),
            pltpu.VMEM((nb, 2 * NY, features), BF16),
            pltpu.VMEM((nb, 2 * NY, features), BF16),
            pltpu.VMEM((2 * NY, features), F32),
            pltpu.VMEM((2 * NY, features), F32),
            pltpu.VMEM((NY, 2, features), BF16),
            pltpu.VMEM((NY, 2, features), BF16),
            pltpu.VMEM((tiles * PAD, DIM), F32),
            pltpu.VMEM((NY, tiles, PAD, DIM), BF16),
            pltpu.VMEM((nb, tiles, PAD, DIM), BF16),
            pltpu.VMEM((ndp, tiles, PAD, DIM), BF16),
            dma((7,)),
            dma((NY,)),
            dma((NY,)),
            dma((n_pieces, nb)),
            dma((n_pieces, nb)),
            dma((CHUNKS, nb)),
            dma((CHUNKS, nb)),
            dma((CHUNKS, NY)),
            dma((CHUNKS, NY)),
            dma((3, most)),
            dma((3, most)),
        ],
        compiler_params=pltpu.CompilerParams(
            collective_id=0, has_side_effects=True, vmem_limit_bytes=52 * 1024 * 1024
        ),
    )(flat(query_proj), flat(key_proj), flat(value_proj), flat(out_grad), pltpu.with_memory_space_constraint(out_gain.reshape(heads, DIM), pltpu.HBM))
    rows = jax.ShapeDtypeStruct((BLOCK, features), BF16)
    outs = pl.pallas_call(
        write_out,
        out_shape=(rows, rows, rows, jax.ShapeDtypeStruct((heads, DIM), F32)),
        in_specs=[vmem] * 4,
        out_specs=(hbm,) * 4,
        scratch_shapes=[dma((4,))],
        compiler_params=pltpu.CompilerParams(vmem_limit_bytes=2 * 1024 * 1024),
    )(*outs)
    shape = (1, BLOCK, features)
    return (outs[0].reshape(shape), outs[1].reshape(shape), outs[2].reshape(shape), outs[3].reshape(features))


def solution(mesh):
    spec = P("dp", "ctx", None)
    return jax.shard_map(
        functools.partial(body, mesh.shape["dp"]),
        mesh=mesh,
        in_specs=(spec, spec, spec, spec, P()),
        out_specs=(spec, spec, spec, P()),
        check_vma=False,
    )
```

```python
import functools
import math

import jax
import jax.numpy as jnp
from jax import lax
from jax.experimental import pallas as pl
from jax.experimental.pallas import tpu as pltpu
from jax.sharding import PartitionSpec as P

DIM = 128
BLOCK = 128
NX, NY, NZ = 4, 8, 2
PAD = 8
MESH = pl.DeviceIdType.MESH
F32 = jnp.float32
BF16 = jnp.bfloat16


def y_order():
    return sorted(range(NY), key=lambda o: (min(o, NY - o), o))


def waves():
    ends = [0, 1, min(5, NY), NY]
    return [(a, b) for a, b in zip(ends, ends[1:]) if a < b]


def dot(a, b, dims):
    return lax.dot_general(a, b, (dims, ((), ())), preferred_element_type=F32)


def kernel(
    heads, ndp,
    q_hbm, k_hbm, v_hbm, g_hbm, gain_hbm,
    gqo, gko, gvo, gg_ref,
    qv, kc, vc, gv, gav, gain_ref, lastk, lastv, st, dpt,
    pg, panel, send, rbuf, acc, pairs, dsend, drecv, gpart, gb1, gb2, gb3,
    insem, a_s, a_r, b_s, b_r, c_s, c_r, d_s, d_r, g_s, g_r,
):
    features = heads * DIM
    nb = NX * NZ
    blocks = NX * NY * NZ
    half = heads // 2
    width = half * DIM
    scale = 1.0 / math.sqrt(DIM)
    escale = scale * math.log2(math.e)
    dp = lax.axis_index("dp")
    me = lax.axis_index("ctx")
    ix = lax.div(me, NY * NZ)
    iy = lax.rem(lax.div(me, NZ), NY)
    iz = lax.rem(me, NZ)
    ib = ix * NZ + iz
    order = y_order()
    slot_of = [order.index(o) for o in range(NY)]

    def y_peer(o):
        return {"ctx": (ix * NY + o) * NZ + iz}

    def b_peer(o):
        return {"ctx": (lax.div(o, NZ) * NY + iy) * NZ + lax.rem(o, NZ)}

    def dp_peer(o):
        return {"dp": o}

    barrier = pltpu.get_barrier_semaphore()

    def greet(device):
        pl.semaphore_signal(barrier, inc=1, device_id=device, device_id_type=MESH)

    for j in order[:0:-1]:
        greet(y_peer(lax.rem(iy + j, NY)))
    for j in range(1, nb):
        greet(b_peer(lax.rem(ib + j, nb)))
    for j in range(1, ndp):
        greet(dp_peer(lax.rem(dp + j, ndp)))

    first = BLOCK - 16
    loads = []

    def load(n, src, dst):
        cp = pltpu.make_async_copy(src, dst, insem.at[n])
        cp.start()
        loads.append(cp)

    load(0, k_hbm.at[pl.ds(first, 16)], kc.at[pl.ds(first, 16)])
    load(1, v_hbm.at[pl.ds(first, 16)], vc.at[pl.ds(first, 16)])
    load(2, k_hbm.at[pl.ds(0, first)], kc.at[pl.ds(0, first)])
    load(3, q_hbm, qv)
    load(4, v_hbm.at[pl.ds(0, first)], vc.at[pl.ds(0, first)])
    load(5, g_hbm, gv)
    load(6, gain_hbm, gain_ref)

    loads[0].wait()
    loads[1].wait()
    ktail = kc[pl.ds(first, 16)].astype(F32)[15:16]
    vtail = vc[pl.ds(first, 16)].astype(F32)[15:16]
    fold = lambda r: jnp.concatenate([r[:, :width], r[:, width:]], axis=0)
    unfold = lambda r: jnp.concatenate([r[0:1], r[1:2]], axis=1)
    panel[ib, 0] = jnp.concatenate([fold(ktail), fold(vtail)], axis=1).astype(BF16)
    gpart[...] = jnp.zeros_like(gpart)

    pl.semaphore_wait(barrier, NY + nb + ndp - 3)

    def a_copy(j, recv):
        p = lax.rem(iy + j, NY)
        s = slot_of[j if recv else NY - j]
        return pltpu.make_async_remote_copy(
            src_ref=panel.at[ib, 0], dst_ref=panel.at[ib, s], send_sem=a_s.at[j], recv_sem=a_r.at[s],
            device_id=y_peer(p), device_id_type=MESH)

    def later(j):
        return lax.div(lax.rem(ib + j, nb), NZ) >= ix

    def earlier(j):
        return lax.div(lax.rem(ib + j, nb), NZ) <= ix

    pieces = [(0, 1, 0, features)]
    for c in range(2):
        for lo, hi in waves()[1:]:
            pieces.append((lo, hi, c * width, width))
    per_chunk = len(waves()) - 1

    def b_copy(n, j, recv):
        lo, hi, start, size = pieces[n]
        p = lax.rem(ib + j, nb)
        s = p if recv else ib
        part = (s, pl.ds(lo, hi - lo), slice(None), pl.ds(start, size))
        return pltpu.make_async_remote_copy(
            src_ref=panel.at[part], dst_ref=panel.at[part],
            send_sem=b_s.at[n, j], recv_sem=b_r.at[n, s],
            device_id=b_peer(p), device_id_type=MESH)

    def send_on(n):
        for j in range(1, nb):
            @pl.when(later(j))
            def _():
                b_copy(n, j, False).start()

    def wave_here(n):
        for s in range(max(1, waves()[n][0]), waves()[n][1]):
            a_copy(order[s], True).wait_recv()

    for j in order[:0:-1]:
        a_copy(j, False).start()
    send_on(0)

    for j in range(1, nb):
        @pl.when(jnp.logical_not(earlier(j)))
        def _():
            panel[lax.rem(ib + j, nb)] = jnp.zeros(panel.shape[1:], BF16)

    key_id = lax.broadcasted_iota(jnp.int32, (BLOCK, BLOCK), 0)
    query_id = lax.broadcasted_iota(jnp.int32, (BLOCK, BLOCK), 1)
    neg = -jnp.inf

    def cols(h):
        return pl.ds(pl.multiple_of(h * DIM, DIM), DIM)

    def local_scores(h, _):
        c = cols(h)
        s = dot(kc[pl.ds(0, BLOCK), c], qv[:, c], ((1,), (1,)))
        st[h, pl.ds(0, BLOCK)] = jnp.where(key_id <= query_id, s, neg)
        return 0

    def local_dprob(h, _):
        c = cols(h)
        ga = (gv[:, c].astype(F32) * gain_ref[pl.ds(h, 1), :]).astype(BF16)
        gav[:, c] = ga
        dpt[h] = dot(vc[pl.ds(0, BLOCK), c], ga, ((1,), (1,)))
        return 0

    loads[2].wait()
    loads[3].wait()
    lax.fori_loop(0, heads, local_scores, 0, unroll=5)
    wave_here(1)
    send_on(1)
    loads[4].wait()
    loads[5].wait()
    loads[6].wait()
    lax.fori_loop(0, heads, local_dprob, 0, unroll=5)

    for n in range(2, len(waves())):
        wave_here(n)
    for n in range(2, len(pieces)):
        send_on(n)

    def sorter(n):
        to_id = lax.broadcasted_iota(jnp.int32, (2 * n, 2 * n), 0)
        from_id = lax.broadcasted_iota(jnp.int32, (2 * n, 2 * n), 1)
        return jnp.where(from_id == 2 * lax.rem(to_id, n) + lax.div(to_id, n), 1.0, 0.0).astype(BF16)

    def chunk(c):
        return pl.ds(c * width, width)

    row = lax.broadcasted_iota(jnp.int32, (blocks, BLOCK), 0)
    off = jnp.zeros_like(row)
    for i in range(1, NY):
        off = jnp.where(lax.rem(row, NY) == i, order[i], off)
    far_id = (lax.div(row, NY * NZ) * NY + lax.rem(iy + off, NY)) * NZ + lax.rem(lax.div(row, NY), NZ)
    far_keep = far_id < me
    far = pl.ds(BLOCK, blocks)

    def take(c):
        for j in range(1, nb):
            @pl.when(earlier(j))
            def _():
                for n in [0] * (c == 0) + [1 + c * per_chunk + w for w in range(per_chunk)]:
                    b_copy(n, j, True).wait_recv()
        rows = dot(sorter(blocks), panel[:, :, :, chunk(c)].reshape(2 * blocks, width), ((1,), (0,))).astype(BF16)
        buf = (kc, vc)[c]
        buf[far, pl.ds(0, width)] = rows[:blocks]
        buf[far, pl.ds(width, width)] = rows[blocks:]

    def keep(start, t, one, two):
        for i in range(nb):
            at = slice(i * NY, (i + 1) * NY)
            send[i, :, pl.ds(pl.multiple_of(start + t * DIM, DIM), DIM)] = (
                jnp.concatenate([one[at], two[at]], axis=0).astype(BF16))

    def fwd(h):
        c = cols(h)
        s_far = jnp.where(far_keep, dot(kc[far, c], qv[:, c], ((1,), (1,))), neg)
        s = jnp.concatenate([st[h, pl.ds(0, BLOCK)], s_far], axis=0)
        top = jnp.max(s, axis=0, keepdims=True)
        e = jnp.exp2((s - top) * escale)
        prob = e * (1.0 / jnp.sum(e, axis=0, keepdims=True))
        st[h] = prob
        both = dot(prob.astype(BF16), jnp.concatenate([gv[:, c], gav[:, c]], axis=1), ((1,), (0,)))
        gpart[pl.ds(h, 1), :] = jnp.sum(vc[pl.ds(0, BLOCK), c].astype(F32) * both[:BLOCK, :DIM], axis=0, keepdims=True)
        pg[:, c] = both[BLOCK:, :DIM]
        gval = both[:, DIM:]
        gvo[:, c] = gval[:BLOCK].astype(BF16)
        lastv[:, c] = gval[first:BLOCK]
        return gval[BLOCK:]

    def bwd(h):
        c = cols(h)
        prob = st[h]
        dprob = jnp.concatenate([dpt[h], dot(vc[far, c], gav[:, c], ((1,), (1,)))], axis=0)
        row_dot = jnp.sum(prob * dprob, axis=0, keepdims=True)
        ds = (prob * (dprob - row_dot)).astype(BF16)
        gkey = dot(ds, qv[:, c], ((1,), (0,))) * scale
        gqo[:, c] = (dot(ds, kc[:, c], ((0,), (0,))) * scale).astype(BF16)
        gko[:, c] = gkey[:BLOCK].astype(BF16)
        lastk[:, c] = gkey[first:BLOCK]
        return gkey[BLOCK:]

    def forward(t, _):
        keep(width, t, fwd(t), fwd(t + half))
        return 0

    def backward(t, _):
        keep(0, t, bwd(t), bwd(t + half))
        return 0

    def far_gain(h, _):
        c = cols(h)
        gpart[pl.ds(h, 1), :] += jnp.sum(vc[far, c].astype(F32) * pg[:, c], axis=0, keepdims=True)
        return 0

    parts = ((width, width), (0, width // 2), (width // 2, width // 2))

    def c_copy(c, j, recv):
        cc = pl.ds(*parts[c])
        p = lax.rem(ib + j, nb)
        s = p if recv else ib
        return pltpu.make_async_remote_copy(
            src_ref=send.at[p, :, cc], dst_ref=rbuf.at[s, :, cc],
            send_sem=c_s.at[c, j], recv_sem=c_r.at[c, s],
            device_id=b_peer(p), device_id_type=MESH)

    gain_groups = ((NY, iy, y_peer, gb1), (nb, ib, b_peer, gb2), (ndp, dp, dp_peer, gb3))

    def gain_copy(stage, j, recv):
        size, mine, where, buf = gain_groups[stage]
        p = lax.rem(mine + j, size)
        s = p if recv else mine
        return pltpu.make_async_remote_copy(
            src_ref=buf.at[s], dst_ref=buf.at[s], send_sem=g_s.at[stage, j], recv_sem=g_r.at[stage, s],
            device_id=where(p), device_id_type=MESH)

    def gain_start(stage, value):
        size, mine, _, buf = gain_groups[stage]
        for t in range(value.shape[0] // PAD):
            buf[mine, t] = value[t * PAD : (t + 1) * PAD].astype(BF16)
        for j in range(1, size):
            gain_copy(stage, j, False).start()

    def gain_end(stage):
        size, _, _, buf = gain_groups[stage]
        for j in range(1, size):
            gain_copy(stage, j, True).wait_recv()
        total = []
        for t in range(buf.shape[1]):
            part = buf[0, t].astype(F32)
            for i in range(1, size):
                part = part + buf[i, t].astype(F32)
            total.append(part)
        return jnp.concatenate(total, axis=0)

    def send_back(c):
        for j in range(1, nb):
            @pl.when(earlier(j))
            def _():
                c_copy(c, j, False).start()

    unroll = half // 2
    take(0)
    lax.fori_loop(0, half, forward, 0, unroll=unroll)
    send_back(0)
    take(1)
    lax.fori_loop(0, heads, far_gain, 0, unroll=heads)
    gain_start(0, gpart[...])
    lax.fori_loop(0, unroll, backward, 0, unroll=unroll)
    send_back(1)
    lax.fori_loop(unroll, half, backward, 0, unroll=unroll)
    send_back(2)

    def d_copy(grp, i, recv):
        p = lax.rem(iy + order[i], NY)
        t = i if recv else slot_of[(NY - order[i]) % NY]
        cc = chunk(grp)
        return pltpu.make_async_remote_copy(
            src_ref=dsend.at[i, :, cc], dst_ref=drecv.at[t, :, cc],
            send_sem=d_s.at[grp, i], recv_sem=d_r.at[grp, t],
            device_id=y_peer(p), device_id_type=MESH)

    def owners(grp):
        cc = chunk(grp)
        acc[:, cc] = send[ib, :, cc].astype(F32)
        for j in range(1, nb):
            @pl.when(later(j))
            def _():
                for c in ((1, 2), (0,))[grp]:
                    c_copy(c, j, True).wait_recv()
                acc[:, cc] += rbuf[lax.rem(ib + j, nb), :, cc].astype(F32)
        pairs[:, cc] = dot(sorter(NY), acc[:, cc].astype(BF16), ((0,), (0,)))
        for i in range(NY):
            dsend[i, :, cc] = pairs[pl.ds(2 * i, 2), cc].astype(BF16)
        for j in range(1, NY):
            d_copy(grp, j, False).start()
        drecv[0, :, cc] = dsend[0, :, cc]

    groups = (1, 0)
    gain_start(1, gain_end(0))
    owners(1)
    owners(0)
    gain_start(2, gain_end(1))
    for grp in groups:
        for j in range(1, NY):
            d_copy(grp, j, True).wait_recv()
    total = drecv[0].astype(F32)
    for i in range(1, NY):
        total = total + drecv[i].astype(F32)
    last = lax.broadcasted_iota(jnp.int32, (16, features), 0) == 15
    gko[pl.ds(first, 16)] = (lastk[...] + jnp.where(last, unfold(total[:, :width]), 0.0)).astype(BF16)
    gvo[pl.ds(first, 16)] = (lastv[...] + jnp.where(last, unfold(total[:, width:]), 0.0)).astype(BF16)

    for j in range(1, NY):
        a_copy(j, False).wait_send()
        for grp in groups:
            d_copy(grp, j, False).wait_send()
    for j in range(1, nb):
        @pl.when(later(j))
        def _():
            for n in range(len(pieces)):
                b_copy(n, j, False).wait_send()

        @pl.when(earlier(j))
        def _():
            for c in range(len(parts)):
                c_copy(c, j, False).wait_send()
    for stage in range(2):
        for j in range(1, gain_groups[stage][0]):
            gain_copy(stage, j, False).wait_send()

    gg_ref[...] = gain_end(2)[:heads] * (1.0 / ndp)
    for j in range(1, ndp):
        gain_copy(2, j, False).wait_send()


def write_out(a, b, c, d, a_hbm, b_hbm, c_hbm, d_hbm, sem):
    copies = [
        pltpu.make_async_copy(src, dst, sem.at[n])
        for n, (src, dst) in enumerate(((a, a_hbm), (b, b_hbm), (c, c_hbm), (d, d_hbm)))
    ]
    for cp in copies:
        cp.start()
    for cp in copies:
        cp.wait()


def body(ndp, query_proj, key_proj, value_proj, out_grad, out_gain):
    features = query_proj.shape[2]
    heads = features // DIM
    nb = NX * NZ
    blocks = NX * NY * NZ
    flat = lambda a: a.reshape(BLOCK, features)
    hbm = pl.BlockSpec(memory_space=pltpu.HBM)
    vmem = pl.BlockSpec(memory_space=pltpu.VMEM)
    dma = pltpu.SemaphoreType.DMA
    most = max(NY, nb, ndp)
    tiles = -(-heads // PAD)
    n_pieces = 1 + (len(waves()) - 1) * 2
    outs = pl.pallas_call(
        functools.partial(kernel, heads, ndp),
        out_shape=(
            pltpu.VMEM((BLOCK, features), BF16),
            pltpu.VMEM((BLOCK, features), BF16),
            pltpu.VMEM((BLOCK, features), BF16),
            pltpu.VMEM((heads, DIM), F32),
        ),
        in_specs=[hbm] * 5,
        out_specs=(vmem,) * 4,
        scratch_shapes=[
            pltpu.VMEM((BLOCK, features), BF16),
            pltpu.VMEM((BLOCK + blocks, features), BF16),
            pltpu.VMEM((BLOCK + blocks, features), BF16),
            pltpu.VMEM((BLOCK, features), BF16),
            pltpu.VMEM((BLOCK, features), BF16),
            pltpu.VMEM((heads, DIM), F32),
            pltpu.VMEM((16, features), F32),
            pltpu.VMEM((16, features), F32),
            pltpu.VMEM((heads, BLOCK + blocks, BLOCK), F32),
            pltpu.VMEM((heads, BLOCK, BLOCK), F32),
            pltpu.VMEM((blocks, features), F32),
            pltpu.VMEM((nb, NY, 2, features), BF16),
            pltpu.VMEM((nb, 2 * NY, features), BF16),
            pltpu.VMEM((nb, 2 * NY, features), BF16),
            pltpu.VMEM((2 * NY, features), F32),
            pltpu.VMEM((2 * NY, features), F32),
            pltpu.VMEM((NY, 2, features), BF16),
            pltpu.VMEM((NY, 2, features), BF16),
            pltpu.VMEM((tiles * PAD, DIM), F32),
            pltpu.VMEM((NY, tiles, PAD, DIM), BF16),
            pltpu.VMEM((nb, tiles, PAD, DIM), BF16),
            pltpu.VMEM((ndp, tiles, PAD, DIM), BF16),
            dma((7,)),
            dma((NY,)),
            dma((NY,)),
            dma((n_pieces, nb)),
            dma((n_pieces, nb)),
            dma((3, nb)),
            dma((3, nb)),
            dma((2, NY)),
            dma((2, NY)),
            dma((3, most)),
            dma((3, most)),
        ],
        compiler_params=pltpu.CompilerParams(
            collective_id=0, has_side_effects=True, vmem_limit_bytes=52 * 1024 * 1024
        ),
    )(flat(query_proj), flat(key_proj), flat(value_proj), flat(out_grad), pltpu.with_memory_space_constraint(out_gain.reshape(heads, DIM), pltpu.HBM))
    rows = jax.ShapeDtypeStruct((BLOCK, features), BF16)
    outs = pl.pallas_call(
        write_out,
        out_shape=(rows, rows, rows, jax.ShapeDtypeStruct((heads, DIM), F32)),
        in_specs=[vmem] * 4,
        out_specs=(hbm,) * 4,
        scratch_shapes=[dma((4,))],
        compiler_params=pltpu.CompilerParams(vmem_limit_bytes=2 * 1024 * 1024),
    )(*outs)
    shape = (1, BLOCK, features)
    return (outs[0].reshape(shape), outs[1].reshape(shape), outs[2].reshape(shape), outs[3].reshape(features))


def solution(mesh):
    spec = P("dp", "ctx", None)
    return jax.shard_map(
        functools.partial(body, mesh.shape["dp"]),
        mesh=mesh,
        in_specs=(spec, spec, spec, spec, P()),
        out_specs=(spec, spec, spec, P()),
        check_vma=False,
    )
```

```python
import functools
import math

import jax
import jax.numpy as jnp
from jax import lax
from jax.experimental import pallas as pl
from jax.experimental.pallas import tpu as pltpu
from jax.sharding import PartitionSpec as P

DIM = 128
BLOCK = 128
NX, NY, NZ = 4, 8, 2
PAD = 8
MESH = pl.DeviceIdType.MESH
F32 = jnp.float32
BF16 = jnp.bfloat16


def y_order():
    return sorted(range(NY), key=lambda o: (min(o, NY - o), o))


def waves():
    ends = [0, 1, min(5, NY), NY]
    return [(a, b) for a, b in zip(ends, ends[1:]) if a < b]


def dot(a, b, dims):
    return lax.dot_general(a, b, (dims, ((), ())), preferred_element_type=F32)


def kernel(
    heads, ndp,
    q_hbm, k_hbm, v_hbm, g_hbm, gain_hbm,
    gqo, gko, gvo, gg_ref,
    qv, kc, vc, gv, gav, gain_ref, lastk, lastv, st, dpt,
    pg, panel, send, rbuf, acc, pairs, dsend, drecv, gpart, gb1, gb2, gb3,
    insem, a_s, a_r, b_s, b_r, c_s, c_r, d_s, d_r, g_s, g_r,
):
    features = heads * DIM
    nb = NX * NZ
    blocks = NX * NY * NZ
    half = heads // 2
    width = half * DIM
    scale = 1.0 / math.sqrt(DIM)
    escale = scale * math.log2(math.e)
    dp = lax.axis_index("dp")
    me = lax.axis_index("ctx")
    ix = lax.div(me, NY * NZ)
    iy = lax.rem(lax.div(me, NZ), NY)
    iz = lax.rem(me, NZ)
    ib = ix * NZ + iz
    order = y_order()
    slot_of = [order.index(o) for o in range(NY)]

    def y_peer(o):
        return {"ctx": (ix * NY + o) * NZ + iz}

    def b_peer(o):
        return {"ctx": (lax.div(o, NZ) * NY + iy) * NZ + lax.rem(o, NZ)}

    def dp_peer(o):
        return {"dp": o}

    barrier = pltpu.get_barrier_semaphore()

    def greet(device):
        pl.semaphore_signal(barrier, inc=1, device_id=device, device_id_type=MESH)

    for j in order[:0:-1]:
        greet(y_peer(lax.rem(iy + j, NY)))
    for j in range(1, nb):
        greet(b_peer(lax.rem(ib + j, nb)))
    for j in range(1, ndp):
        greet(dp_peer(lax.rem(dp + j, ndp)))

    first = BLOCK - 16
    loads = []

    def load(n, src, dst):
        cp = pltpu.make_async_copy(src, dst, insem.at[n])
        cp.start()
        loads.append(cp)

    load(0, k_hbm.at[pl.ds(first, 16)], kc.at[pl.ds(first, 16)])
    load(1, v_hbm.at[pl.ds(first, 16)], vc.at[pl.ds(first, 16)])
    load(2, k_hbm.at[pl.ds(0, first)], kc.at[pl.ds(0, first)])
    load(3, q_hbm, qv)
    load(4, v_hbm.at[pl.ds(0, first)], vc.at[pl.ds(0, first)])
    load(5, g_hbm, gv)
    load(6, gain_hbm, gain_ref)

    loads[0].wait()
    loads[1].wait()
    ktail = kc[pl.ds(first, 16)].astype(F32)[15:16]
    vtail = vc[pl.ds(first, 16)].astype(F32)[15:16]
    fold = lambda r: jnp.concatenate([r[:, :width], r[:, width:]], axis=0)
    unfold = lambda r: jnp.concatenate([r[0:1], r[1:2]], axis=1)
    panel[ib, 0] = jnp.concatenate([fold(ktail), fold(vtail)], axis=1).astype(BF16)
    gpart[...] = jnp.zeros_like(gpart)

    pl.semaphore_wait(barrier, NY + nb + ndp - 3)

    def a_copy(j, recv):
        p = lax.rem(iy + j, NY)
        s = slot_of[j if recv else NY - j]
        return pltpu.make_async_remote_copy(
            src_ref=panel.at[ib, 0], dst_ref=panel.at[ib, s], send_sem=a_s.at[j], recv_sem=a_r.at[s],
            device_id=y_peer(p), device_id_type=MESH)

    def later(j):
        return lax.div(lax.rem(ib + j, nb), NZ) >= ix

    def earlier(j):
        return lax.div(lax.rem(ib + j, nb), NZ) <= ix

    pieces = [(0, 1, 0, features)]
    for c in range(2):
        for lo, hi in waves()[1:]:
            pieces.append((lo, hi, c * width, width))
    per_chunk = len(waves()) - 1

    def b_copy(n, j, recv):
        lo, hi, start, size = pieces[n]
        p = lax.rem(ib + j, nb)
        s = p if recv else ib
        part = (s, pl.ds(lo, hi - lo), slice(None), pl.ds(start, size))
        return pltpu.make_async_remote_copy(
            src_ref=panel.at[part], dst_ref=panel.at[part],
            send_sem=b_s.at[n, j], recv_sem=b_r.at[n, s],
            device_id=b_peer(p), device_id_type=MESH)

    def send_on(n):
        for j in range(1, nb):
            @pl.when(later(j))
            def _():
                b_copy(n, j, False).start()

    def wave_here(n):
        for s in range(max(1, waves()[n][0]), waves()[n][1]):
            a_copy(order[s], True).wait_recv()

    for j in order[:0:-1]:
        a_copy(j, False).start()
    send_on(0)

    for j in range(1, nb):
        @pl.when(jnp.logical_not(earlier(j)))
        def _():
            panel[lax.rem(ib + j, nb)] = jnp.zeros(panel.shape[1:], BF16)

    key_id = lax.broadcasted_iota(jnp.int32, (BLOCK, BLOCK), 0)
    query_id = lax.broadcasted_iota(jnp.int32, (BLOCK, BLOCK), 1)
    neg = -jnp.inf

    def cols(h):
        return pl.ds(pl.multiple_of(h * DIM, DIM), DIM)

    def local_scores(h, _):
        c = cols(h)
        s = dot(kc[pl.ds(0, BLOCK), c], qv[:, c], ((1,), (1,)))
        st[h, pl.ds(0, BLOCK)] = jnp.where(key_id <= query_id, s, neg)
        return 0

    def local_dprob(h, _):
        c = cols(h)
        ga = (gv[:, c].astype(F32) * gain_ref[pl.ds(h, 1), :]).astype(BF16)
        gav[:, c] = ga
        dpt[h] = dot(vc[pl.ds(0, BLOCK), c], ga, ((1,), (1,)))
        return 0

    loads[2].wait()
    loads[3].wait()
    lax.fori_loop(0, heads, local_scores, 0, unroll=5)
    wave_here(1)
    send_on(1)
    loads[4].wait()
    loads[5].wait()
    loads[6].wait()
    lax.fori_loop(0, heads, local_dprob, 0, unroll=5)

    for n in range(2, len(waves())):
        wave_here(n)
    for n in range(2, len(pieces)):
        send_on(n)

    def sorter(n):
        to_id = lax.broadcasted_iota(jnp.int32, (2 * n, 2 * n), 0)
        from_id = lax.broadcasted_iota(jnp.int32, (2 * n, 2 * n), 1)
        return jnp.where(from_id == 2 * lax.rem(to_id, n) + lax.div(to_id, n), 1.0, 0.0).astype(BF16)

    def chunk(c):
        return pl.ds(c * width, width)

    row = lax.broadcasted_iota(jnp.int32, (blocks, BLOCK), 0)
    off = jnp.zeros_like(row)
    for i in range(1, NY):
        off = jnp.where(lax.rem(row, NY) == i, order[i], off)
    far_id = (lax.div(row, NY * NZ) * NY + lax.rem(iy + off, NY)) * NZ + lax.rem(lax.div(row, NY), NZ)
    far_keep = far_id < me
    far = pl.ds(BLOCK, blocks)

    def take(c):
        for j in range(1, nb):
            @pl.when(earlier(j))
            def _():
                for n in [0] * (c == 0) + [1 + c * per_chunk + w for w in range(per_chunk)]:
                    b_copy(n, j, True).wait_recv()
        rows = dot(sorter(blocks), panel[:, :, :, chunk(c)].reshape(2 * blocks, width), ((1,), (0,))).astype(BF16)
        buf = (kc, vc)[c]
        buf[far, pl.ds(0, width)] = rows[:blocks]
        buf[far, pl.ds(width, width)] = rows[blocks:]

    def keep(start, t, one, two):
        for i in range(nb):
            at = slice(i * NY, (i + 1) * NY)
            send[i, :, pl.ds(pl.multiple_of(start + t * DIM, DIM), DIM)] = (
                jnp.concatenate([one[at], two[at]], axis=0).astype(BF16))

    def fwd(h):
        c = cols(h)
        s_far = jnp.where(far_keep, dot(kc[far, c], qv[:, c], ((1,), (1,))), neg)
        s = jnp.concatenate([st[h, pl.ds(0, BLOCK)], s_far], axis=0)
        top = jnp.max(s, axis=0, keepdims=True)
        e = jnp.exp2((s - top) * escale)
        prob = e * (1.0 / jnp.sum(e, axis=0, keepdims=True))
        st[h] = prob
        both = dot(prob.astype(BF16), jnp.concatenate([gv[:, c], gav[:, c]], axis=1), ((1,), (0,)))
        gpart[pl.ds(h, 1), :] = jnp.sum(vc[pl.ds(0, BLOCK), c].astype(F32) * both[:BLOCK, :DIM], axis=0, keepdims=True)
        pg[:, c] = both[BLOCK:, :DIM]
        gval = both[:, DIM:]
        gvo[:, c] = gval[:BLOCK].astype(BF16)
        lastv[:, c] = gval[first:BLOCK]
        return gval[BLOCK:]

    def bwd(h):
        c = cols(h)
        prob = st[h]
        dprob = jnp.concatenate([dpt[h], dot(vc[far, c], gav[:, c], ((1,), (1,)))], axis=0)
        row_dot = jnp.sum(prob * dprob, axis=0, keepdims=True)
        ds = (prob * (dprob - row_dot)).astype(BF16)
        gkey = dot(ds, qv[:, c], ((1,), (0,))) * scale
        gqo[:, c] = (dot(ds, kc[:, c], ((0,), (0,))) * scale).astype(BF16)
        gko[:, c] = gkey[:BLOCK].astype(BF16)
        lastk[:, c] = gkey[first:BLOCK]
        return gkey[BLOCK:]

    def forward(t, _):
        keep(width, t, fwd(t), fwd(t + half))
        return 0

    def backward(t, _):
        keep(0, t, bwd(t), bwd(t + half))
        return 0

    def far_gain(h, _):
        c = cols(h)
        gpart[pl.ds(h, 1), :] += jnp.sum(vc[far, c].astype(F32) * pg[:, c], axis=0, keepdims=True)
        return 0

    parts = ((width, width), (0, width // 2), (width // 2, width // 2))

    def c_copy(c, j, recv):
        cc = pl.ds(*parts[c])
        p = lax.rem(ib + j, nb)
        s = p if recv else ib
        return pltpu.make_async_remote_copy(
            src_ref=send.at[p, :, cc], dst_ref=rbuf.at[s, :, cc],
            send_sem=c_s.at[c, j], recv_sem=c_r.at[c, s],
            device_id=b_peer(p), device_id_type=MESH)

    gain_groups = ((NY, iy, y_peer, gb1), (nb, ib, b_peer, gb2), (ndp, dp, dp_peer, gb3))

    def gain_copy(stage, j, recv):
        size, mine, where, buf = gain_groups[stage]
        p = lax.rem(mine + j, size)
        s = p if recv else mine
        return pltpu.make_async_remote_copy(
            src_ref=buf.at[s], dst_ref=buf.at[s], send_sem=g_s.at[stage, j], recv_sem=g_r.at[stage, s],
            device_id=where(p), device_id_type=MESH)

    def gain_start(stage, value):
        size, mine, _, buf = gain_groups[stage]
        for t in range(value.shape[0] // PAD):
            buf[mine, t] = value[t * PAD : (t + 1) * PAD].astype(BF16)
        for j in range(1, size):
            gain_copy(stage, j, False).start()

    def gain_end(stage):
        size, _, _, buf = gain_groups[stage]
        for j in range(1, size):
            gain_copy(stage, j, True).wait_recv()
        total = []
        for t in range(buf.shape[1]):
            part = buf[0, t].astype(F32)
            for i in range(1, size):
                part = part + buf[i, t].astype(F32)
            total.append(part)
        return jnp.concatenate(total, axis=0)

    def send_back(c):
        for j in range(1, nb):
            @pl.when(earlier(j))
            def _():
                c_copy(c, j, False).start()

    unroll = half // 2
    take(0)
    lax.fori_loop(0, half, forward, 0, unroll=half)
    send_back(0)
    take(1)
    lax.fori_loop(0, heads, far_gain, 0, unroll=heads)
    gain_start(0, gpart[...])
    lax.fori_loop(0, unroll, backward, 0, unroll=unroll)
    send_back(1)
    lax.fori_loop(unroll, half, backward, 0, unroll=unroll)
    send_back(2)

    def d_copy(grp, i, recv):
        p = lax.rem(iy + order[i], NY)
        t = i if recv else slot_of[(NY - order[i]) % NY]
        cc = chunk(grp)
        return pltpu.make_async_remote_copy(
            src_ref=dsend.at[i, :, cc], dst_ref=drecv.at[t, :, cc],
            send_sem=d_s.at[grp, i], recv_sem=d_r.at[grp, t],
            device_id=y_peer(p), device_id_type=MESH)

    def owners(grp):
        cc = chunk(grp)
        acc[:, cc] = send[ib, :, cc].astype(F32)
        for j in range(1, nb):
            @pl.when(later(j))
            def _():
                for c in ((1, 2), (0,))[grp]:
                    c_copy(c, j, True).wait_recv()
                acc[:, cc] += rbuf[lax.rem(ib + j, nb), :, cc].astype(F32)
        pairs[:, cc] = dot(sorter(NY), acc[:, cc].astype(BF16), ((0,), (0,)))
        for i in range(NY):
            dsend[i, :, cc] = pairs[pl.ds(2 * i, 2), cc].astype(BF16)
        for j in range(1, NY):
            d_copy(grp, j, False).start()
        drecv[0, :, cc] = dsend[0, :, cc]

    groups = (1, 0)
    gain_start(1, gain_end(0))
    owners(1)
    owners(0)
    gain_start(2, gain_end(1))
    for grp in groups:
        for j in range(1, NY):
            d_copy(grp, j, True).wait_recv()
    total = drecv[0].astype(F32)
    for i in range(1, NY):
        total = total + drecv[i].astype(F32)
    last = lax.broadcasted_iota(jnp.int32, (16, features), 0) == 15
    gko[pl.ds(first, 16)] = (lastk[...] + jnp.where(last, unfold(total[:, :width]), 0.0)).astype(BF16)
    gvo[pl.ds(first, 16)] = (lastv[...] + jnp.where(last, unfold(total[:, width:]), 0.0)).astype(BF16)

    for j in range(1, NY):
        a_copy(j, False).wait_send()
        for grp in groups:
            d_copy(grp, j, False).wait_send()
    for j in range(1, nb):
        @pl.when(later(j))
        def _():
            for n in range(len(pieces)):
                b_copy(n, j, False).wait_send()

        @pl.when(earlier(j))
        def _():
            for c in range(len(parts)):
                c_copy(c, j, False).wait_send()
    for stage in range(2):
        for j in range(1, gain_groups[stage][0]):
            gain_copy(stage, j, False).wait_send()

    gg_ref[...] = gain_end(2)[:heads] * (1.0 / ndp)
    for j in range(1, ndp):
        gain_copy(2, j, False).wait_send()


def write_out(a, b, c, d, a_hbm, b_hbm, c_hbm, d_hbm, sem):
    copies = [
        pltpu.make_async_copy(src, dst, sem.at[n])
        for n, (src, dst) in enumerate(((a, a_hbm), (b, b_hbm), (c, c_hbm), (d, d_hbm)))
    ]
    for cp in copies:
        cp.start()
    for cp in copies:
        cp.wait()


def body(ndp, query_proj, key_proj, value_proj, out_grad, out_gain):
    features = query_proj.shape[2]
    heads = features // DIM
    nb = NX * NZ
    blocks = NX * NY * NZ
    flat = lambda a: a.reshape(BLOCK, features)
    hbm = pl.BlockSpec(memory_space=pltpu.HBM)
    vmem = pl.BlockSpec(memory_space=pltpu.VMEM)
    dma = pltpu.SemaphoreType.DMA
    most = max(NY, nb, ndp)
    tiles = -(-heads // PAD)
    n_pieces = 1 + (len(waves()) - 1) * 2
    outs = pl.pallas_call(
        functools.partial(kernel, heads, ndp),
        out_shape=(
            pltpu.VMEM((BLOCK, features), BF16),
            pltpu.VMEM((BLOCK, features), BF16),
            pltpu.VMEM((BLOCK, features), BF16),
            pltpu.VMEM((heads, DIM), F32),
        ),
        in_specs=[hbm] * 5,
        out_specs=(vmem,) * 4,
        scratch_shapes=[
            pltpu.VMEM((BLOCK, features), BF16),
            pltpu.VMEM((BLOCK + blocks, features), BF16),
            pltpu.VMEM((BLOCK + blocks, features), BF16),
            pltpu.VMEM((BLOCK, features), BF16),
            pltpu.VMEM((BLOCK, features), BF16),
            pltpu.VMEM((heads, DIM), F32),
            pltpu.VMEM((16, features), F32),
            pltpu.VMEM((16, features), F32),
            pltpu.VMEM((heads, BLOCK + blocks, BLOCK), F32),
            pltpu.VMEM((heads, BLOCK, BLOCK), F32),
            pltpu.VMEM((blocks, features), F32),
            pltpu.VMEM((nb, NY, 2, features), BF16),
            pltpu.VMEM((nb, 2 * NY, features), BF16),
            pltpu.VMEM((nb, 2 * NY, features), BF16),
            pltpu.VMEM((2 * NY, features), F32),
            pltpu.VMEM((2 * NY, features), F32),
            pltpu.VMEM((NY, 2, features), BF16),
            pltpu.VMEM((NY, 2, features), BF16),
            pltpu.VMEM((tiles * PAD, DIM), F32),
            pltpu.VMEM((NY, tiles, PAD, DIM), BF16),
            pltpu.VMEM((nb, tiles, PAD, DIM), BF16),
            pltpu.VMEM((ndp, tiles, PAD, DIM), BF16),
            dma((7,)),
            dma((NY,)),
            dma((NY,)),
            dma((n_pieces, nb)),
            dma((n_pieces, nb)),
            dma((3, nb)),
            dma((3, nb)),
            dma((2, NY)),
            dma((2, NY)),
            dma((3, most)),
            dma((3, most)),
        ],
        compiler_params=pltpu.CompilerParams(
            collective_id=0, has_side_effects=True, vmem_limit_bytes=52 * 1024 * 1024
        ),
    )(flat(query_proj), flat(key_proj), flat(value_proj), flat(out_grad), pltpu.with_memory_space_constraint(out_gain.reshape(heads, DIM), pltpu.HBM))
    rows = jax.ShapeDtypeStruct((BLOCK, features), BF16)
    outs = pl.pallas_call(
        write_out,
        out_shape=(rows, rows, rows, jax.ShapeDtypeStruct((heads, DIM), F32)),
        in_specs=[vmem] * 4,
        out_specs=(hbm,) * 4,
        scratch_shapes=[dma((4,))],
        compiler_params=pltpu.CompilerParams(vmem_limit_bytes=2 * 1024 * 1024),
    )(*outs)
    shape = (1, BLOCK, features)
    return (outs[0].reshape(shape), outs[1].reshape(shape), outs[2].reshape(shape), outs[3].reshape(features))


def solution(mesh):
    spec = P("dp", "ctx", None)
    return jax.shard_map(
        functools.partial(body, mesh.shape["dp"]),
        mesh=mesh,
        in_specs=(spec, spec, spec, spec, P()),
        out_specs=(spec, spec, spec, P()),
        check_vma=False,
    )
```
